256 devices in a mesh: gx: 4 (over y), gy: 8 (over z_hi, core), gz: 8 (over z_lo, x).
Axes of the slice: x: 4, y: 4, z: 8 (z_hi: 4, z_lo: 2; z = z_hi * 2 + z_lo), core: 2. Of those that a mesh axis runs over, the one named last changes fastest.
Arguments:
- density: float32 [16, 128, 2048], P('gx', 'gy', 'gz'), may hold values from 2 to 8
- energy: float32 [16, 128, 2048], P('gx', 'gy', 'gz'), may hold values from 0.2 to 1.5
- velocity: float32 [3, 16, 128, 2048], P(None, 'gx', 'gy', 'gz'), may hold values from -3 to 3
- plastic_strain: float32 [16, 128, 2048], P('gx', 'gy', 'gz'), may hold values from 0.01 to 0.5
- damage: float32 [16, 128, 2048], P('gx', 'gy', 'gz'), may hold values from 0 to 0.5
- deviator: float32 [6, 16, 128, 2048], P(None, 'gx', 'gy', 'gz'), may hold values from -1.2 to 1.2
- materials: int32 [16, 128, 2048], P('gx', 'gy', 'gz'), may hold values from 0 to 2
- timestep: float32 [2], replicated, may hold values from 0.05 to 0.3
Outputs:
- density_out: float32 [16, 128, 2048], P('gx', 'gy', 'gz')
- energy_out: float32 [16, 128, 2048], P('gx', 'gy', 'gz')
- velocity_out: float32 [3, 16, 128, 2048], P(None, 'gx', 'gy', 'gz')
- plastic_out: float32 [16, 128, 2048], P('gx', 'gy', 'gz')
- damage_out: float32 [16, 128, 2048], P('gx', 'gy', 'gz')
- deviator_out: float32 [6, 16, 128, 2048], P(None, 'gx', 'gy', 'gz')
The draws below stay inside these ranges and needn't reach their ends.
All inputs are finite; a program needn't handle non-finite values. Where the reference program divides by a largest or mean magnitude, that divisor is 1e-20 or more.
Results may differ from the reference program's by a relative error of at most 0.0003.
Values sent between devices are 32-bit elements; how exact they have to be, the bound alone decides.
No kernel may reach another device: no remote copies, remote signals or barrier semaphores. Data moves between devices by JAX's collectives and lax.ppermute only.
A program may use at most 128 MiB of HBM per device.

```python
import math
import jax
import jax.numpy as jnp
from jax import lax

STEPS = 2
NX = 16
NY = 128
NZ = 2048


def touch_ends(entries, rng, least, top_value):
    dims = entries.shape
    spot = [jax.random.randint(jax.random.fold_in(rng, axis), (), 0, dims[axis]) for axis in range(len(dims))]
    entries = entries.at[tuple(spot)].set(least)
    longest = dims.index(max(dims))
    spot[longest] = (spot[longest] + 1) % dims[longest]
    return entries.at[tuple(spot)].set(top_value)


def levels(key, dims, split, least, high):
    def one(axis_at, parts):
        draws = jax.random.uniform(jax.random.fold_in(jax.random.fold_in(key, 6), axis_at), (parts,), jnp.float32, least / len(split), high / len(split))
        return jnp.repeat(jnp.exp(draws), dims[axis_at] // parts).reshape((-1,) + (1,) * (len(dims) - axis_at - 1))

    gain = one(*split[0])
    for cut in split[1:]:
        gain = gain * one(*cut)
    return gain


def scatter_about(stream_key, shape, width, reach, pieces=(), held_as=jnp.bfloat16):
    array = jax.random.normal(stream_key, shape, jnp.float32) * width
    if len(pieces) > 0:
        array = levels(stream_key, shape, pieces, -0.22, 0.18) * array
    return jnp.clip(array, min=-reach, max=reach).astype(held_as)


def setup_inputs(seed: int = 0) -> dict:
    key_list = jax.random.split(jax.random.key(seed), 9)
    density = jnp.clip(2.0 + 6.0 * jax.random.uniform(key_list[0], (NX, NY, NZ), jnp.float32) ** levels(key_list[0], (NX, NY, NZ), ((0, 4), (1, 8), (2, 8)), -0.2, 0.2), 2.0, 8.0)
    energy = jnp.clip(0.2 + 1.3 * jax.random.uniform(key_list[1], (NX, NY, NZ), jnp.float32) ** levels(key_list[1], (NX, NY, NZ), ((0, 4), (1, 8), (2, 8)), -0.2, 0.2), 0.2, 1.5)
    velocity = scatter_about(key_list[2], (3, NX, NY, NZ), 0.5, 3.0, ((1, 4), (2, 8), (3, 8)), jnp.float32)
    plastic_strain = jnp.clip(jnp.exp(math.log(0.5) - 3.912023 * jax.random.uniform(key_list[3], (NX, NY, NZ), jnp.float32) ** levels(key_list[3], (NX, NY, NZ), ((0, 4), (1, 8), (2, 8)), -0.2, 0.2)), 0.01, 0.5)
    damage = jnp.clip(0.5 * jax.random.uniform(key_list[4], (NX, NY, NZ), jnp.float32) ** levels(key_list[4], (NX, NY, NZ), ((0, 4), (1, 8), (2, 8)), -0.2, 0.2), 0.0, 0.5)
    deviator = scatter_about(key_list[5], (6, NX, NY, NZ), 0.2, 1.2, ((1, 4), (2, 8), (3, 8)), jnp.float32)
    materials = touch_ends(jax.random.randint(key_list[6], (NX, NY, NZ), 0, 3), jax.random.fold_in(key_list[6], 1), 0, 2).astype(jnp.int32)
    timestep = jnp.clip(jax.random.uniform(key_list[7], (STEPS,), jnp.float32, 0.05, 0.3), 0.05, 0.3)
    return {"density": density, "energy": energy, "velocity": velocity, "plastic_strain": plastic_strain, "damage": damage, "deviator": deviator, "materials": materials, "timestep": timestep}


shear_table = (1.0, 0.5, 0.8)
sound_table = (1.5, 1.2, 1.0)
gruneisen_table = (2.0, 2.1, 1.9)
rest_table = (4.0, 3.0, 5.0)
yield_table = (0.3, 0.2, 0.25)
harden_table = (0.5, 0.3, 0.4)
exponent_table = (0.3, 0.4, 0.35)
rate_table = (0.02, 0.015, 0.01)
cfl_number = 0.2

def lookup(kind_values, values_table):
    result = jnp.zeros(kind_values.shape, jnp.float32)
    for material_no in range(3):
        result = result + jnp.where(kind_values == material_no, values_table[material_no], 0.0)
    return result

def material_params(kind_values):
    return (lookup(kind_values, shear_table), lookup(kind_values, yield_table), lookup(kind_values, harden_table), lookup(kind_values, exponent_table), lookup(kind_values, rate_table))

def central(padded, direction):
    upper_cut = [slice(1, -1)] * 3
    lower_cut = [slice(1, -1)] * 3
    upper_cut[direction] = slice(2, None)
    lower_cut[direction] = slice(None, -2)
    return 0.5 * (padded[tuple(upper_cut)] - padded[tuple(lower_cut)])

def interior(padded):
    return padded[..., 1:-1, 1:-1, 1:-1]

def stress_update(vel_padded, deviator, plastic, damage, pressure, params, time_step):
    shear_mod, yield_base, harden_mod, harden_exp, rate_coef = params
    gradient = [[central(vel_padded[comp_a], comp_b) for comp_b in range(3)] for comp_a in range(3)]
    diverge = gradient[0][0] + gradient[1][1] + gradient[2][2]
    third_div = diverge / 3.0
    strain = [gradient[0][0] - third_div, gradient[1][1] - third_div, gradient[2][2] - third_div, 0.5 * (gradient[0][1] + gradient[1][0]), 0.5 * (gradient[1][2] + gradient[2][1]), 0.5 * (gradient[0][2] + gradient[2][0])]
    trial_dev = [deviator[comp_k] + 2.0 * shear_mod * time_step * strain[comp_k] for comp_k in range(6)]
    trial_sq = trial_dev[0] ** 2 + trial_dev[1] ** 2 + trial_dev[2] ** 2 + 2.0 * (trial_dev[3] ** 2 + trial_dev[4] ** 2 + trial_dev[5] ** 2)
    equivalent = jnp.sqrt(1.5 * trial_sq)
    strain_sq = strain[0] ** 2 + strain[1] ** 2 + strain[2] ** 2 + 2.0 * (strain[3] ** 2 + strain[4] ** 2 + strain[5] ** 2)
    strain_rate = jnp.sqrt(strain_sq * (2.0 / 3.0))
    flow_stress = (yield_base + harden_mod * jnp.exp(harden_exp * jnp.log(plastic))) * (1.0 + rate_coef * jnp.log1p(strain_rate)) * (1.0 - damage)
    bound_stress = jnp.maximum(equivalent, flow_stress)
    factor = flow_stress / bound_stress
    increment = (bound_stress - flow_stress) / (3.0 * shear_mod)
    triaxial = jnp.clip(-pressure / bound_stress, -1.5, 1.5)
    failure = 0.05 + 0.8 * jnp.exp(-1.5 * triaxial)
    new_plastic = plastic + increment
    new_damage = jnp.minimum(damage + increment / failure, 0.9)
    new_dev = [trial_dev[comp_k] * factor for comp_k in range(6)]
    stress = [new_dev[0] - pressure, new_dev[1] - pressure, new_dev[2] - pressure, new_dev[3], new_dev[4], new_dev[5]]
    work_rate = stress[0] * gradient[0][0] + stress[1] * gradient[1][1] + stress[2] * gradient[2][2] + 2.0 * (stress[3] * strain[3] + stress[4] * strain[4] + stress[5] * strain[5])
    return (jnp.stack(stress), jnp.stack(new_dev), new_plastic, new_damage, work_rate)

def finish(stress_padded, density, energy, velocity, work_rate, time_step):
    force_x = central(stress_padded[0], 0) + central(stress_padded[3], 1) + central(stress_padded[5], 2)
    force_y = central(stress_padded[3], 0) + central(stress_padded[1], 1) + central(stress_padded[4], 2)
    force_z = central(stress_padded[5], 0) + central(stress_padded[4], 1) + central(stress_padded[2], 2)
    new_velocity = velocity + time_step * jnp.stack([force_x, force_y, force_z]) / density
    new_energy = energy + time_step * work_rate / density
    return (new_velocity, new_energy)

def sweep(padded, sweep_axis, time_step, lower_wall, upper_wall):
    array_dim = sweep_axis + 1
    length = padded.shape[array_dim] - 4

    def cut_along(source, offset, extent):
        return lax.slice_in_dim(source, offset, offset + extent, axis=array_dim)
    density = padded[0:1]
    conserved = jnp.concatenate([density, density * padded[1:]], axis=0)
    differ = cut_along(conserved, 1, length + 3) - cut_along(conserved, 0, length + 3)
    back_diff = cut_along(differ, 0, length + 2)
    fore_diff = cut_along(differ, 1, length + 2)
    product = back_diff * fore_diff
    positive = product > 0.0
    slopes = jnp.where(positive, 2.0 * product / (back_diff + fore_diff + jnp.where(positive, 0.0, 1.0)), 0.0)
    vel_row = padded[2 + sweep_axis:3 + sweep_axis]
    face_speed = 0.5 * (cut_along(vel_row, 1, length + 1) + cut_along(vel_row, 2, length + 1))
    courant = time_step * face_speed
    left_flux = face_speed * (cut_along(conserved, 1, length + 1) + 0.5 * (1.0 - courant) * cut_along(slopes, 0, length + 1))
    right_flux = face_speed * (cut_along(conserved, 2, length + 1) - 0.5 * (1.0 + courant) * cut_along(slopes, 1, length + 1))
    face_flux = jnp.where(face_speed > 0.0, left_flux, right_flux)
    dims_shape = [1, 1, 1, 1]
    dims_shape[array_dim] = length + 1
    face_index = jnp.arange(length + 1, dtype=jnp.int32).reshape(dims_shape)
    closed = (face_index == 0) & lower_wall | (face_index == length) & upper_wall
    face_flux = jnp.where(closed, 0.0, face_flux)
    return cut_along(conserved, 2, length) - time_step * (cut_along(face_flux, 1, length) - cut_along(face_flux, 0, length))

def to_primitive(updated, inside):
    density = updated[0:1]
    safe_density = jnp.where(inside, density, 1.0)
    return jnp.where(inside, jnp.concatenate([density, updated[1:] / safe_density], axis=0), 0.0)

def reference(density, energy, velocity, plastic_strain, damage, deviator, materials, timestep):
    sound_speed = lookup(materials, sound_table)
    gruneisen = lookup(materials, gruneisen_table)
    rest_density = lookup(materials, rest_table)
    params = material_params(materials)
    for step_no in range(STEPS):
        top_speed = jnp.max(lax.optimization_barrier(jnp.max(jnp.abs(velocity), axis=0)) + sound_speed)
        time_step = timestep[step_no] / (1.0 + timestep[step_no] * top_speed / cfl_number)
        pressure = sound_speed * sound_speed * (density - rest_density) + gruneisen * density * energy
        vel_padded = jnp.pad(velocity, ((0, 0), (1, 1), (1, 1), (1, 1)))
        stress, deviator, plastic_strain, damage, work_rate = stress_update(vel_padded, deviator, plastic_strain, damage, pressure, params, time_step)
        stress_padded = jnp.pad(stress, ((0, 0), (1, 1), (1, 1), (1, 1)))
        velocity, energy = finish(stress_padded, density, energy, velocity, work_rate, time_step)
        primitive = jnp.concatenate([density[None], energy[None], velocity, plastic_strain[None], damage[None], deviator], axis=0)
        for sweep_axis in range(3):
            widths = [(0, 0), (0, 0), (0, 0), (0, 0)]
            widths[sweep_axis + 1] = (2, 2)
            primitive = to_primitive(sweep(jnp.pad(primitive, widths), sweep_axis, time_step, True, True), True)
        density = primitive[0]
        energy = primitive[1]
        velocity = primitive[2:5]
        plastic_strain = primitive[5]
        damage = primitive[6]
        deviator = primitive[7:13]
    return (density, energy, velocity, plastic_strain, damage, deviator)
```

```python
import jax
import jax.numpy as jnp
from jax import lax
from jax.sharding import PartitionSpec as P

STEPS = 2


shear_table = (1.0, 0.5, 0.8)
sound_table = (1.5, 1.2, 1.0)
gruneisen_table = (2.0, 2.1, 1.9)
rest_table = (4.0, 3.0, 5.0)
yield_table = (0.3, 0.2, 0.25)
harden_table = (0.5, 0.3, 0.4)
exponent_table = (0.3, 0.4, 0.35)
rate_table = (0.02, 0.015, 0.01)
cfl_number = 0.2


ALL_AXES = ("gx", "gy", "gz")


def ring(count, step):
    return [(i, (i + step) % count) for i in range(count)]


def swap_faces(to_high, to_low, axis):
    count = lax.axis_size(axis)
    place = lax.axis_index(axis)
    low = lax.ppermute(to_high, axis, ring(count, 1))
    high = lax.ppermute(to_low, axis, ring(count, -1))
    return jnp.where(place == 0, 0.0, low), jnp.where(place == count - 1, 0.0, high)


def cut(block, dim, start, size):
    if start < 0:
        start += block.shape[dim]
    return lax.slice_in_dim(block, start, start + size, axis=dim)


def global_max(value):
    total = lax.axis_size("gx") * lax.axis_size("gy") * lax.axis_size("gz")
    rows = jnp.full((total, 128), value, jnp.float32)
    return jnp.max(lax.all_to_all(rows, ALL_AXES, 0, 0))


def faces(block, axis, dim):
    return swap_faces(cut(block, dim, -1, 1), cut(block, dim, 0, 1), axis)


def faces_z(block, axis, width):
    lead = block.shape[:-1]
    def pack(face):
        return jnp.moveaxis(face, -1, 0).reshape(width * lead[0], -1)
    def unpack(face):
        return jnp.moveaxis(face.reshape((width,) + lead), 0, -1)
    low, high = swap_faces(
        pack(cut(block, block.ndim - 1, -width, width)), pack(cut(block, block.ndim - 1, 0, width)), axis
    )
    return unpack(low), unpack(high)


def lookup(kind_values, values_table):
    result = jnp.zeros(kind_values.shape, jnp.float32)
    for material_no in range(3):
        result = result + jnp.where(kind_values == material_no, values_table[material_no], 0.0)
    return result


def material_params(kind_values):
    return (
        lookup(kind_values, shear_table),
        lookup(kind_values, yield_table),
        lookup(kind_values, harden_table),
        lookup(kind_values, exponent_table),
        lookup(kind_values, rate_table),
    )


def central(block, pair, direction):
    low, high = pair
    length = block.shape[direction]
    upper = jnp.concatenate([cut(block, direction, 1, length - 1), high], axis=direction)
    lower = jnp.concatenate([low, cut(block, direction, 0, length - 1)], axis=direction)
    return 0.5 * (upper - lower)


def stress_update(velocity, vel_faces, deviator, plastic, damage, pressure, params, time_step):
    shear_mod, yield_base, harden_mod, harden_exp, rate_coef = params
    gradient = [
        [
            central(
                velocity[comp_a], (vel_faces[comp_b][0][comp_a], vel_faces[comp_b][1][comp_a]), comp_b
            )
            for comp_b in range(3)
        ]
        for comp_a in range(3)
    ]
    diverge = gradient[0][0] + gradient[1][1] + gradient[2][2]
    third_div = diverge / 3.0
    strain = [
        gradient[0][0] - third_div,
        gradient[1][1] - third_div,
        gradient[2][2] - third_div,
        0.5 * (gradient[0][1] + gradient[1][0]),
        0.5 * (gradient[1][2] + gradient[2][1]),
        0.5 * (gradient[0][2] + gradient[2][0]),
    ]
    trial_dev = [
        deviator[comp_k] + 2.0 * shear_mod * time_step * strain[comp_k] for comp_k in range(6)
    ]
    trial_sq = (
        trial_dev[0] ** 2
        + trial_dev[1] ** 2
        + trial_dev[2] ** 2
        + 2.0 * (trial_dev[3] ** 2 + trial_dev[4] ** 2 + trial_dev[5] ** 2)
    )
    equivalent = jnp.sqrt(1.5 * trial_sq)
    strain_sq = (
        strain[0] ** 2
        + strain[1] ** 2
        + strain[2] ** 2
        + 2.0 * (strain[3] ** 2 + strain[4] ** 2 + strain[5] ** 2)
    )
    strain_rate = jnp.sqrt(strain_sq * (2.0 / 3.0))
    flow_stress = (
        (yield_base + harden_mod * jnp.exp(harden_exp * jnp.log(plastic)))
        * (1.0 + rate_coef * jnp.log1p(strain_rate))
        * (1.0 - damage)
    )
    bound_stress = jnp.maximum(equivalent, flow_stress)
    factor = flow_stress / bound_stress
    increment = (bound_stress - flow_stress) / (3.0 * shear_mod)
    triaxial = jnp.clip(-pressure / bound_stress, -1.5, 1.5)
    failure = 0.05 + 0.8 * jnp.exp(-1.5 * triaxial)
    new_plastic = plastic + increment
    new_damage = jnp.minimum(damage + increment / failure, 0.9)
    new_dev = [trial_dev[comp_k] * factor for comp_k in range(6)]
    stress = [
        new_dev[0] - pressure,
        new_dev[1] - pressure,
        new_dev[2] - pressure,
        new_dev[3],
        new_dev[4],
        new_dev[5],
    ]
    work_rate = (
        stress[0] * gradient[0][0]
        + stress[1] * gradient[1][1]
        + stress[2] * gradient[2][2]
        + 2.0 * (stress[3] * strain[3] + stress[4] * strain[4] + stress[5] * strain[5])
    )
    return (jnp.stack(stress), jnp.stack(new_dev), new_plastic, new_damage, work_rate)


ACROSS = ((0, 3, 5), (3, 1, 4), (5, 4, 2))


def finish(stress, stress_faces, density, velocity, time_step):
    force = []
    for comp in range(3):
        total = 0.0
        for direction in range(3):
            low, high = stress_faces[direction]
            total = total + central(
                stress[ACROSS[direction][comp]], (low[comp], high[comp]), direction
            )
        force.append(total)
    return velocity + time_step * jnp.stack(force) / density


def sweep(padded, sweep_axis, time_step, lower_wall, upper_wall):
    array_dim = sweep_axis + 1
    length = padded.shape[array_dim] - 4

    def cut_along(source, offset, extent):
        return lax.slice_in_dim(source, offset, offset + extent, axis=array_dim)

    density = padded[0:1]
    conserved = jnp.concatenate([density, density * padded[1:]], axis=0)
    differ = cut_along(conserved, 1, length + 3) - cut_along(conserved, 0, length + 3)
    back_diff = cut_along(differ, 0, length + 2)
    fore_diff = cut_along(differ, 1, length + 2)
    product = back_diff * fore_diff
    positive = product > 0.0
    slopes = jnp.where(
        positive, 2.0 * product / (back_diff + fore_diff + jnp.where(positive, 0.0, 1.0)), 0.0
    )
    vel_row = padded[2 + sweep_axis : 3 + sweep_axis]
    face_speed = 0.5 * (cut_along(vel_row, 1, length + 1) + cut_along(vel_row, 2, length + 1))
    courant = time_step * face_speed
    left_flux = face_speed * (
        cut_along(conserved, 1, length + 1)
        + 0.5 * (1.0 - courant) * cut_along(slopes, 0, length + 1)
    )
    right_flux = face_speed * (
        cut_along(conserved, 2, length + 1)
        - 0.5 * (1.0 + courant) * cut_along(slopes, 1, length + 1)
    )
    face_flux = jnp.where(face_speed > 0.0, left_flux, right_flux)
    dims_shape = [1, 1, 1, 1]
    dims_shape[array_dim] = length + 1
    face_index = jnp.arange(length + 1, dtype=jnp.int32).reshape(dims_shape)
    closed = (face_index == 0) & lower_wall | (face_index == length) & upper_wall
    face_flux = jnp.where(closed, 0.0, face_flux)
    return cut_along(conserved, 2, length) - time_step * (
        cut_along(face_flux, 1, length) - cut_along(face_flux, 0, length)
    )


def to_primitive(updated):
    density = updated[0:1]
    safe_density = jnp.where(True, density, 1.0)
    return jnp.where(True, jnp.concatenate([density, updated[1:] / safe_density], axis=0), 0.0)


def shards(density, energy, velocity, plastic_strain, damage, deviator, materials, timestep):
    place_x = lax.axis_index("gx")
    place_y = lax.axis_index("gy")
    place_z = lax.axis_index("gz")
    groups_x = lax.axis_size("gx")
    groups_y = lax.axis_size("gy")
    groups_z = lax.axis_size("gz")
    kind_float = materials.astype(jnp.float32)
    sound_speed = lookup(kind_float, sound_table)
    gruneisen = lookup(kind_float, gruneisen_table)
    rest_density = lookup(kind_float, rest_table)
    params = material_params(kind_float)
    for step_no in range(STEPS):
        vel_faces = [
            faces(velocity, "gx", 1),
            faces(velocity, "gy", 2),
            faces_z(velocity, "gz", 1),
        ]
        top_speed = global_max(jnp.max(jnp.max(jnp.abs(velocity), axis=0) + sound_speed))
        time_step = timestep[step_no] / (1.0 + timestep[step_no] * top_speed / cfl_number)
        pressure = (
            sound_speed * sound_speed * (density - rest_density) + gruneisen * density * energy
        )
        stress, deviator, plastic_strain, damage, work_rate = stress_update(
            velocity, vel_faces, deviator, plastic_strain, damage, pressure, params, time_step
        )
        energy = energy + time_step * work_rate / density
        early = jnp.concatenate(
            [density[None], energy[None], plastic_strain[None], damage[None], deviator], axis=0
        )
        sx = jnp.stack([stress[k] for k in ACROSS[0]])
        sy = jnp.stack([stress[k] for k in ACROSS[1]])
        sz = jnp.stack([stress[k] for k in ACROSS[2]])
        def layers(block, start, size):
            return cut(block, 1, start, size).reshape((-1,) + block.shape[2:])
        x_low, x_high = swap_faces(
            jnp.concatenate([layers(sx, -1, 1), layers(early, -2, 2)]),
            jnp.concatenate([layers(sx, 0, 1), layers(early, 0, 2)]),
            "gx",
        )
        stress_faces = [
            (x_low[:3][:, None], x_high[:3][:, None]),
            faces(sy, "gy", 2),
            faces_z(sz, "gz", 1),
        ]
        early_low = x_low[3:].reshape((10, 2) + x_low.shape[1:])
        early_high = x_high[3:].reshape((10, 2) + x_high.shape[1:])
        velocity = finish(stress, stress_faces, density, velocity, time_step)
        v_low, v_high = swap_faces(cut(velocity, 1, -2, 2), cut(velocity, 1, 0, 2), "gx")
        def order(part, vel):
            return [part[:2], vel, part[2:]]
        low = jnp.concatenate(order(early_low, v_low))
        high = jnp.concatenate(order(early_high, v_high))
        padded = jnp.concatenate([low, jnp.concatenate(order(early, velocity)), high], axis=1)
        primitive = to_primitive(sweep(padded, 0, time_step, place_x == 0, place_x == groups_x - 1))
        low, high = swap_faces(cut(primitive, 2, -2, 2), cut(primitive, 2, 0, 2), "gy")
        padded = jnp.concatenate([low, primitive, high], axis=2)
        primitive = to_primitive(sweep(padded, 1, time_step, place_y == 0, place_y == groups_y - 1))
        low, high = faces_z(primitive, "gz", 2)
        padded = jnp.concatenate([low, primitive, high], axis=3)
        primitive = to_primitive(sweep(padded, 2, time_step, place_z == 0, place_z == groups_z - 1))
        density = primitive[0]
        energy = primitive[1]
        velocity = primitive[2:5]
        plastic_strain = primitive[5]
        damage = primitive[6]
        deviator = primitive[7:13]
    return (density, energy, velocity, plastic_strain, damage, deviator)


def solution(mesh):
    placed = (
        P("gx", "gy", "gz"),
        P("gx", "gy", "gz"),
        P(None, "gx", "gy", "gz"),
        P("gx", "gy", "gz"),
        P("gx", "gy", "gz"),
        P(None, "gx", "gy", "gz"),
        P("gx", "gy", "gz"),
        P(),
    )
    return jax.shard_map(
        shards,
        mesh=mesh,
        in_specs=placed,
        out_specs=(
            P("gx", "gy", "gz"),
            P("gx", "gy", "gz"),
            P(None, "gx", "gy", "gz"),
            P("gx", "gy", "gz"),
            P("gx", "gy", "gz"),
            P(None, "gx", "gy", "gz"),
        ),
        check_vma=False,
    )
```

```python
import jax
import jax.numpy as jnp
from jax import lax
from jax.experimental import pallas as pl
from jax.experimental.pallas import tpu as pltpu
from jax.sharding import PartitionSpec as P


FIELDS = 13
PLANES = 16
ROWS = 24
OWN = 16
LANES = 128
HALF = 64
PAD = 2

shear_table = (1.0, 0.5, 0.8)
sound_table = (1.5, 1.2, 1.0)
gruneisen_table = (2.0, 2.1, 1.9)
rest_table = (4.0, 3.0, 5.0)
yield_table = (0.3, 0.2, 0.25)
harden_table = (0.5, 0.3, 0.4)
exponent_table = (0.3, 0.4, 0.35)
rate_table = (0.02, 0.015, 0.01)
cfl_number = 0.2

ALL_AXES = ("gx", "gy", "gz")
ACROSS = ((0, 3, 5), (3, 1, 4), (5, 4, 2))


def roll(value, shift, axis):
    shift = shift % value.shape[axis]
    return value if shift == 0 else pltpu.roll(value, shift, axis)


def iota(shape, axis):
    return lax.broadcasted_iota(jnp.int32, shape, axis)


def inverse(value):
    guess = pl.reciprocal(value, approx=True)
    return guess * (2.0 - value * guess)


def pick(first, second, table):
    return jnp.where(first, table[0], jnp.where(second, table[1], table[2]))


def stack_rows(even, odd, upper):
    low_rows = iota((8, LANES), 0) < 4
    if upper:
        return jnp.where(low_rows, roll(even[8:], 4, 0), odd[8:])
    return jnp.where(low_rows, even[:8], roll(odd[:8], 4, 0))


def halo_tile(high, low, odd):
    low_rows = iota((8, LANES), 0) < 4
    if odd:
        return jnp.where(low_rows, roll(high, 4, 0), low)
    return jnp.where(low_rows, high, roll(low, 4, 0))


def pack_kernel(place, dens, ener, vel, plas, dama, devi, mat, own, to1, to2, to3, top):
    me = place[0]
    refs = [dens, ener] + [vel.at[i] for i in range(3)] + [plas, dama]
    refs = refs + [devi.at[i] for i in range(6)] + [mat]
    peak = None
    for x in range(4):
        for t in range(2):
            cols = slice(t * LANES, (t + 1) * LANES)
            speed = jnp.maximum(jnp.abs(vel[0, x, :, cols]), jnp.abs(vel[1, x, :, cols]))
            speed = jnp.maximum(speed, jnp.abs(vel[2, x, :, cols]))
            kind = mat[x, :, cols]
            speed = speed + pick(kind == 0, kind == 1, sound_table)
            peak = speed if peak is None else jnp.maximum(peak, speed)
    top[...] = jnp.full(top.shape, jnp.max(peak), jnp.float32)
    left = iota((OWN, LANES), 1) < HALF
    for k, out in enumerate((own, to1, to2, to3)):
        target = me ^ k
        cols = pl.ds(pl.multiple_of((target >> 1) * LANES, LANES), LANES)
        odd = target & 1
        for f in range(FIELDS + 1):
            for j in range(2):
                even_plane = refs[f][2 * j, :, cols].astype(jnp.float32)
                odd_plane = refs[f][2 * j + 1, :, cols].astype(jnp.float32)
                out[f, j] = jnp.where(
                    left,
                    pltpu.roll(even_plane, odd * HALF, 1),
                    pltpu.roll(odd_plane, (1 - odd) * HALF, 1),
                )


def spread_kernel(place, own, from1, from2, from3, state, up, down):
    me = place[0]
    for k, src in enumerate((own, from1, from2, from3)):
        block = me ^ k
        for f in range(FIELDS + 1):
            first, second = src[f, 0], src[f, 1]
            state[f, 4 * block] = first
            state[f, 4 * block + 1] = roll(first, HALF, 1)
            state[f, 4 * block + 2] = second
            state[f, 4 * block + 3] = roll(second, HALF, 1)
            up[f, block] = stack_rows(first, second, True)
            down[f, block] = stack_rows(first, second, False)


def rows_kernel(state, low, high, tiles, z_up, z_down):
    for f in range(FIELDS + 1):
        for block in range(4):
            for j in range(2):
                tile = halo_tile(high[f, block], low[f, block], j == 1)
                tiles[f, 4 * block + 2 * j] = tile
                tiles[f, 4 * block + 2 * j + 1] = roll(tile, HALF, 1)

    def plane(p, carry):
        for rows in (OWN, 8):
            group = iota((rows, LANES), 1) >> 3
            ups = jnp.zeros((rows, LANES), jnp.float32)
            downs = ups
            for f in range(FIELDS + 1):
                value = state[f, p] if rows == OWN else tiles[f, p]
                ups = jnp.where(group == f, roll(value, 8 * f - (HALF - 8), 1), ups)
                downs = jnp.where(group == f, roll(value, 8 * f, 1), downs)
            at = slice(0, OWN) if rows == OWN else slice(OWN, ROWS)
            z_up[p, at] = ups
            z_down[p, at] = downs
        return carry

    lax.fori_loop(0, PLANES, plane, 0)


def set_masks(place, width, inside, face_y, face_z):
    shape = (ROWS, LANES)
    row, lane = iota(shape, 0), iota(shape, 1)
    row_ok = (row < OWN) | ((row < OWN + 4) & (place[1] < place[3])) | ((row >= OWN + 4) & (place[1] > 0))
    lane_ok = (
        (lane < HALF)
        | ((lane < HALF + width) & (place[2] < place[4]))
        | ((lane >= LANES - width) & (place[2] > 0))
    )
    ok = jnp.where(row_ok & lane_ok, 1.0, 0.0)
    inside[...] = ok
    face_y[...] = ok * roll(ok, -1, 0)
    face_z[...] = ok * roll(ok, -1, 1)


def step_size(step_no, timestep, tops):
    top_speed = jnp.max(tops[...], axis=0, keepdims=True)
    asked = timestep[step_no]
    return asked / (1.0 + asked * top_speed / cfl_number)


def central(upper, lower):
    return 0.5 * (upper - lower)


def limited(back, fore):
    product = back * fore
    return jnp.where(product > 0.0, product * inverse(back + fore), 0.0)


def carried(positive, here, there, slope_here, slope_there, courant, weight):
    return courant * (
        jnp.where(positive, here, there) + weight * jnp.where(positive, slope_here, slope_there)
    )


def weigh(courant):
    return jnp.where(courant > 0.0, 1.0, -1.0) - courant


def rolled_sweep(fields, comp, courant_mask, inside, axis, dt):
    velocity = fields[comp]
    courant = dt * 0.5 * (velocity + roll(velocity, -1, axis)) * courant_mask
    positive = courant > 0.0
    weight = weigh(courant)
    density = fields[0]
    result = []
    scale = None
    for f in range(FIELDS):
        q = density if f == 0 else density * fields[f]
        q_next = roll(q, -1, axis)
        fore = q_next - q
        slope = limited(roll(fore, 1, axis), fore)
        flux = carried(positive, q, q_next, slope, roll(slope, -1, axis), courant, weight)
        q = q - (flux - roll(flux, 1, axis))
        if f == 0:
            scale = jnp.where(inside, inverse(q), 0.0)
            result.append(jnp.where(inside, q, 0.0))
        else:
            result.append(q * scale)
    return result


def advance(dt, state, moved, stress, courants, weights, scales, inside, face_y, face_z, out):
    def strain_plane(p, carry):
        at = p + PAD
        ok = inside[...] > 0.0
        vel = [state[2 + i, at] for i in range(3)]
        grad = [
            [
                central(state[2 + i, at + 1], state[2 + i, at - 1]),
                central(roll(vel[i], -1, 0), roll(vel[i], 1, 0)),
                central(roll(vel[i], -1, 1), roll(vel[i], 1, 1)),
            ]
            for i in range(3)
        ]
        third_div = (grad[0][0] + grad[1][1] + grad[2][2]) * (1.0 / 3.0)
        strain = [
            grad[0][0] - third_div,
            grad[1][1] - third_div,
            grad[2][2] - third_div,
            0.5 * (grad[0][1] + grad[1][0]),
            0.5 * (grad[1][2] + grad[2][1]),
            0.5 * (grad[0][2] + grad[2][0]),
        ]
        kind = state[FIELDS, at]
        first, second = kind == 0.0, kind == 1.0
        density, energy = state[0, at], state[1, at]
        plastic, damage = state[5, at], state[6, at]
        pressure = (
            pick(first, second, tuple(c * c for c in sound_table))
            * (density - pick(first, second, rest_table))
            + pick(first, second, gruneisen_table) * density * energy
        )
        shear_dt = pick(first, second, tuple(2.0 * g for g in shear_table)) * dt
        trial = [state[7 + k, at] + shear_dt * strain[k] for k in range(6)]
        trial_sq = (
            trial[0] * trial[0]
            + trial[1] * trial[1]
            + trial[2] * trial[2]
            + 2.0 * (trial[3] * trial[3] + trial[4] * trial[4] + trial[5] * trial[5])
        )
        strain_sq = (
            strain[0] * strain[0]
            + strain[1] * strain[1]
            + strain[2] * strain[2]
            + 2.0 * (strain[3] * strain[3] + strain[4] * strain[4] + strain[5] * strain[5])
        )
        equivalent = jnp.sqrt(1.5 * trial_sq)
        strain_rate = jnp.sqrt(strain_sq * (2.0 / 3.0))
        hardened = pick(first, second, yield_table) + pick(first, second, harden_table) * jnp.exp(
            pick(first, second, exponent_table) * jnp.log(plastic)
        )
        flow = (
            hardened
            * (1.0 + pick(first, second, rate_table) * jnp.log(1.0 + strain_rate))
            * (1.0 - damage)
        )
        bound = jnp.maximum(equivalent, flow)
        per_bound = inverse(bound)
        factor = flow * per_bound
        increment = (bound - flow) * pick(first, second, tuple(1.0 / (3.0 * g) for g in shear_table))
        triaxial = jnp.clip(-pressure * per_bound, -1.5, 1.5)
        failure = 0.05 + 0.8 * jnp.exp(-1.5 * triaxial)
        state[5, at] = jnp.where(ok, plastic + increment, 0.0)
        state[6, at] = jnp.where(ok, jnp.minimum(damage + increment * inverse(failure), 0.9), 0.0)
        dev = [jnp.where(ok, trial[k] * factor, 0.0) for k in range(6)]
        held = jnp.where(ok, pressure, 0.0)
        full = [dev[0] - held, dev[1] - held, dev[2] - held, dev[3], dev[4], dev[5]]
        for k in range(6):
            state[7 + k, at] = dev[k]
            stress[k, p + 1] = full[k]
        work = (
            full[0] * grad[0][0]
            + full[1] * grad[1][1]
            + full[2] * grad[2][2]
            + 2.0 * (full[3] * strain[3] + full[4] * strain[4] + full[5] * strain[5])
        )
        state[1, at] = jnp.where(ok, energy + dt * work * inverse(density), 0.0)
        return carry

    zero = jnp.zeros((ROWS, LANES), jnp.float32)
    for k in range(6):
        stress[k, 0] = zero
        stress[k, PLANES + 1] = zero
    lax.fori_loop(0, PLANES, strain_plane, 0)

    def force_plane(p, carry):
        at = p + PAD
        ok = inside[...] > 0.0
        pushed = jnp.where(ok, dt * inverse(state[0, at]), 0.0)
        here = [stress[k, p + 1] for k in range(6)]
        for i in range(3):
            along_x, along_y, along_z = ACROSS[0][i], ACROSS[1][i], ACROSS[2][i]
            force = (
                central(stress[along_x, p + 2], stress[along_x, p])
                + central(roll(here[along_y], -1, 0), roll(here[along_y], 1, 0))
                + central(roll(here[along_z], -1, 1), roll(here[along_z], 1, 1))
            )
            state[2 + i, at] = state[2 + i, at] + pushed * force
        return carry

    lax.fori_loop(0, PLANES, force_plane, 0)

    for p in range(PLANES - 1):
        courant = dt * 0.5 * (state[2, p + PAD] + state[2, p + PAD + 1])
        courants[p] = courant
        weights[p] = weigh(courant)

    def stream(load, store):
        here = load(0)
        back = here
        ahead = load(1)
        fore = ahead - here
        slope = limited(back, fore)
        last_flux = None
        for p in range(PLANES):
            if p < PLANES - 1:
                further = load(p + 2) if p + 2 < PLANES else None
                next_fore = further - ahead if further is not None else -ahead
                next_slope = limited(fore, next_fore)
                courant = courants[p]
                flux = carried(
                    courant > 0.0, here, ahead, slope, next_slope, courant, weights[p]
                )
                change = flux if last_flux is None else flux - last_flux
            else:
                flux, further, next_fore, next_slope = None, None, None, None
                change = -last_flux
            store(p, here - change)
            last_flux, here, ahead, fore, slope = flux, ahead, further, next_fore, next_slope

    def store_density(p, value):
        ok = inside[...] > 0.0
        moved[0, p] = jnp.where(ok, value, 0.0)
        scales[p] = jnp.where(ok, inverse(value), 0.0)

    stream(lambda p: state[0, p + PAD], store_density)

    def field(f, carry):
        def store(p, value):
            moved[f, p] = value * scales[p]

        stream(lambda p: state[0, p + PAD] * state[f, p + PAD], store)
        return carry

    lax.fori_loop(1, FIELDS, field, 0)

    def plane(p, carry):
        ok = inside[...] > 0.0
        fields = rolled_sweep([moved[f, p] for f in range(FIELDS)], 3, face_y[...], ok, 0, dt)
        fields = [value[:OWN] for value in fields]
        fields = rolled_sweep(fields, 4, face_z[:OWN], ok[:OWN], 1, dt)
        for f in range(FIELDS):
            out[f, p] = fields[f]
        return carry

    lax.fori_loop(0, PLANES, plane, 0)


def clear_ends(state):
    zero = jnp.zeros((ROWS, LANES), jnp.float32)
    for f in range(FIELDS + 1):
        for p in (0, 1, PLANES + PAD, PLANES + PAD + 1):
            state[f, p] = zero


def first_kernel(
    place, timestep, tops, own, tiles, z_low, z_high, out, kinds, up, down, top,
    state, moved, stress, courants, weights, scales, inside, face_y, face_z,
):
    set_masks(place, 8, inside, face_y, face_z)
    clear_ends(state)
    dt = step_size(0, timestep, tops)

    def gather(p, carry):
        ok = inside[...] > 0.0
        lane = iota((ROWS, LANES), 1)
        below, above = z_low[p], z_high[p]
        for f in range(FIELDS + 1):
            value = jnp.concatenate([own[f, p], tiles[f, p]], axis=0)
            side = jnp.where(lane < 96, roll(above, HALF - 8 * f, 1), roll(below, LANES - 8 - 8 * f, 1))
            value = jnp.where(ok, jnp.where(lane < HALF, value, side), 0.0)
            state[f, p + PAD] = value
            if f == FIELDS:
                kinds[p] = value
        return carry

    lax.fori_loop(0, PLANES, gather, 0)
    advance(dt, state, moved, stress, courants, weights, scales, inside, face_y, face_z, out)

    lane = iota((OWN, LANES), 1)
    peak = jnp.zeros((OWN, LANES), jnp.float32)

    def peaks(p, peak):
        speed = jnp.maximum(jnp.abs(out[2, p]), jnp.abs(out[3, p]))
        speed = jnp.maximum(speed, jnp.abs(out[4, p]))
        kind = kinds[p, :OWN]
        speed = speed + pick(kind == 0.0, kind == 1.0, sound_table)
        return jnp.maximum(peak, jnp.where(lane < HALF, speed, 0.0))

    peak = lax.fori_loop(0, PLANES, peaks, peak)
    top[...] = jnp.full(top.shape, jnp.max(peak), jnp.float32)

    def messages(i, carry):
        for f in range(FIELDS):
            even, odd = out[f, 2 * i], out[f, 2 * i + 1]
            up[f, i] = stack_rows(even, odd, True)
            down[f, i] = stack_rows(even, odd, False)
        return carry

    lax.fori_loop(0, PLANES // 2, messages, 0)


def second_kernel(
    place, timestep, tops, own, kinds, low, high, mine, to1, to2, to3,
    state, moved, stress, courants, weights, scales, inside, face_y, face_z, out,
):
    set_masks(place, 4, inside, face_y, face_z)
    clear_ends(state)
    dt = step_size(1, timestep, tops)

    def gather(i, carry):
        ok = inside[...] > 0.0
        for f in range(FIELDS):
            for odd in range(2):
                p = 2 * i + odd
                tile = halo_tile(high[f, i], low[f, i], odd == 1)
                value = jnp.concatenate([own[f, p], tile], axis=0)
                state[f, p + PAD] = jnp.where(ok, value, 0.0)
        for odd in range(2):
            state[FIELDS, 2 * i + odd + PAD] = kinds[2 * i + odd]
        return carry

    lax.fori_loop(0, PLANES // 2, gather, 0)
    advance(dt, state, moved, stress, courants, weights, scales, inside, face_y, face_z, out)

    left = iota((OWN, LANES), 1) < HALF
    for k, dest in enumerate((mine, to1, to2, to3)):
        block = place[0] ^ k
        for f in range(FIELDS):
            for j in range(2):
                even, odd = out[f, 4 * block + 2 * j], out[f, 4 * block + 2 * j + 1]
                dest[f, j] = jnp.where(left, even, roll(odd, HALF, 1))


def unpack_kernel(place, mine, from1, from2, from3, dens, ener, vel, plas, dama, devi, held):
    me = place[0]
    refs = [dens, ener] + [vel.at[i] for i in range(3)] + [plas, dama]
    refs = refs + [devi.at[i] for i in range(6)]
    for k, src in enumerate((mine, from1, from2, from3)):
        held[me ^ k] = src[...]
    left = iota((OWN, LANES), 1) < HALF
    for f in range(FIELDS):
        for j in range(2):
            for t in range(2):
                first, second = held[2 * t, f, j], held[2 * t + 1, f, j]
                cols = slice(t * LANES, (t + 1) * LANES)
                refs[f][2 * j, :, cols] = jnp.where(left, first, roll(second, HALF, 1))
                refs[f][2 * j + 1, :, cols] = jnp.where(left, roll(first, HALF, 1), second)


IN_VMEM = pl.BlockSpec(memory_space=pltpu.VMEM)
IN_SMEM = pl.BlockSpec(memory_space=pltpu.SMEM)


def call(kernel, scalars, outs, scratch, *args):
    return pl.pallas_call(
        kernel,
        out_shape=[jax.ShapeDtypeStruct(shape, jnp.float32) for shape in outs],
        in_specs=[IN_SMEM] * scalars + [IN_VMEM] * (len(args) - scalars),
        out_specs=[IN_VMEM] * len(outs),
        scratch_shapes=[pltpu.VMEM(shape, jnp.float32) for shape in scratch],
        compiler_params=pltpu.CompilerParams(vmem_limit_bytes=48 * 1024 * 1024),
    )(*args)


def ring_pair(to_next, to_last, axes, order):
    after = order[1:] + order[:1]
    low = lax.ppermute(to_next, axes, list(zip(order, after)))
    high = lax.ppermute(to_last, axes, list(zip(after, order)))
    return low, high


def swap_blocks(parts):
    count = lax.axis_size("gx")
    return [
        lax.ppermute(part, "gx", [(i, i ^ (k + 1)) for i in range(count)])
        for k, part in enumerate(parts)
    ]


def shards(density, energy, velocity, plastic_strain, damage, deviator, materials, timestep):
    size_x, size_y, size_z = lax.axis_size("gx"), lax.axis_size("gy"), lax.axis_size("gz")
    place_x, place_y, place_z = lax.axis_index("gx"), lax.axis_index("gy"), lax.axis_index("gz")
    total = size_x * size_y * size_z
    chunks = size_z * size_x
    place = jnp.stack(
        [place_x, place_y, place_z * size_x + place_x, jnp.int32(size_y - 1), jnp.int32(chunks - 1)]
    ).astype(jnp.int32)
    z_order = [x * size_z + z for z in range(size_z) for x in range(size_x)]
    all_fields = FIELDS + 1
    part = (all_fields, 2, OWN, LANES)
    own, *parts, top = call(
        pack_kernel, 1, [part] * 4 + [(total, LANES)], [],
        place, density, energy, velocity, plastic_strain, damage, deviator, materials,
    )
    parts = swap_blocks(parts)
    tops = lax.all_to_all(top, ALL_AXES, 0, 0)
    state, up, down = call(
        spread_kernel,
        1,
        [(all_fields, PLANES, OWN, LANES)] + [(all_fields, 4, 8, LANES)] * 2,
        [],
        place,
        own,
        *parts,
    )
    low, high = ring_pair(up, down, "gy", list(range(size_y)))
    tiles, z_up, z_down = call(
        rows_kernel,
        0,
        [(all_fields, PLANES, 8, LANES)] + [(PLANES, ROWS, LANES)] * 2,
        [],
        state,
        low,
        high,
    )
    z_low, z_high = ring_pair(z_up, z_down, ("gx", "gz"), z_order)
    full = (ROWS, LANES)
    scratch = [
        (all_fields, PLANES + 2 * PAD) + full,
        (FIELDS, PLANES) + full,
        (6, PLANES + 2) + full,
        (PLANES,) + full,
        (PLANES,) + full,
        (PLANES,) + full,
        full,
        full,
        full,
    ]
    block = (FIELDS, PLANES, OWN, LANES)
    state, kinds, up, down, top = call(
        first_kernel,
        2,
        [block, (PLANES,) + full] + [(FIELDS, PLANES // 2, 8, LANES)] * 2 + [(total, LANES)],
        scratch,
        place,
        timestep,
        tops,
        state,
        tiles,
        z_low,
        z_high,
    )
    low, high = ring_pair(up, down, "gy", list(range(size_y)))
    tops = lax.all_to_all(top, ALL_AXES, 0, 0)
    mine, *parts = call(
        second_kernel,
        2,
        [(FIELDS, 2, OWN, LANES)] * 4,
        scratch + [block],
        place,
        timestep,
        tops,
        state,
        kinds,
        low,
        high,
    )
    parts = swap_blocks(parts)
    cells = density.shape
    return tuple(
        call(
            unpack_kernel,
            1,
            [cells, cells, (3,) + cells, cells, cells, (6,) + cells],
            [(4, FIELDS, 2, OWN, LANES)],
            place,
            mine,
            *parts,
        )
    )


def solution(mesh):
    cells = P("gx", "gy", "gz")
    vectors = P(None, "gx", "gy", "gz")
    return jax.shard_map(
        shards,
        mesh=mesh,
        in_specs=(cells, cells, vectors, cells, cells, vectors, cells, P()),
        out_specs=(cells, cells, vectors, cells, cells, vectors),
        check_vma=False,
    )
```

```python
import jax
import jax.numpy as jnp
from jax import lax
from jax.experimental import pallas as pl
from jax.experimental.pallas import tpu as pltpu
from jax.sharding import PartitionSpec as P


FIELDS = 13
PLANES = 16
ROWS = 24
OWN = 16
LANES = 128
HALF = 64
PAD = 2

shear_table = (1.0, 0.5, 0.8)
sound_table = (1.5, 1.2, 1.0)
gruneisen_table = (2.0, 2.1, 1.9)
rest_table = (4.0, 3.0, 5.0)
yield_table = (0.3, 0.2, 0.25)
harden_table = (0.5, 0.3, 0.4)
exponent_table = (0.3, 0.4, 0.35)
rate_table = (0.02, 0.015, 0.01)
cfl_number = 0.2

PACK_LIMIT = 62 * 1024 * 1024
ACROSS = ((0, 3, 5), (3, 1, 4), (5, 4, 2))


def roll(value, shift, axis):
    shift = shift % value.shape[axis]
    return value if shift == 0 else pltpu.roll(value, shift, axis)


def position():
    size_x = lax.axis_size("gx")
    place_x = lax.axis_index("gx")
    chunk = lax.axis_index("gz") * size_x + place_x
    return place_x, lax.axis_index("gy"), chunk, lax.axis_size("gy") - 1, size_x * lax.axis_size("gz") - 1


def iota(shape, axis):
    return lax.broadcasted_iota(jnp.int32, shape, axis)


def inverse(value):
    guess = pl.reciprocal(value, approx=True)
    return guess * (2.0 - value * guess)


def pick(first, second, table):
    return jnp.where(first, table[0], jnp.where(second, table[1], table[2]))


def stack_rows(even, odd, upper):
    low_rows = iota((8, LANES), 0) < 4
    if upper:
        return jnp.where(low_rows, roll(even[8:], 4, 0), odd[8:])
    return jnp.where(low_rows, even[:8], roll(odd[:8], 4, 0))


def halo_tile(high, low, odd):
    low_rows = iota((8, LANES), 0) < 4
    if odd:
        return jnp.where(low_rows, roll(high, 4, 0), low)
    return jnp.where(low_rows, high, roll(low, 4, 0))


PART_ROWS = (FIELDS + 1) * 2 * OWN


def part_rows(f, j):
    return slice((2 * f + j) * OWN, (2 * f + j + 1) * OWN)


def pack_kernel(*args):
    sources, (own, to1, to2, to3, edges, z_up, z_down) = args[:7], args[7:14]
    buffers, arrived = args[14:21], args[21]
    copies = [
        pltpu.make_async_copy(source, buffer, arrived.at[i])
        for i, (source, buffer) in enumerate(zip(sources, buffers))
    ]
    for copy in copies:
        copy.start()
    for copy in copies:
        copy.wait()
    dens, ener, vel, plas, dama, devi, mat = buffers
    me = position()[0]
    refs = [dens, ener] + [vel.at[i] for i in range(3)] + [plas, dama]
    refs = refs + [devi.at[i] for i in range(6)] + [mat]
    peak = None
    for x in range(4):
        for t in range(2):
            cols = slice(t * LANES, (t + 1) * LANES)
            speed = jnp.maximum(jnp.abs(vel[0, x, :, cols]), jnp.abs(vel[1, x, :, cols]))
            speed = jnp.maximum(speed, jnp.abs(vel[2, x, :, cols]))
            kind = mat[x, :, cols]
            speed = speed + pick(kind == 0, kind == 1, sound_table)
            peak = speed if peak is None else jnp.maximum(peak, speed)
    peak = jnp.full((8, LANES), jnp.max(peak), jnp.float32)
    left = iota((OWN, LANES), 1) < HALF
    for k, out in enumerate((own, to1, to2, to3)):
        out[PART_ROWS:] = peak
        target = me ^ k
        cols = pl.ds(pl.multiple_of((target >> 1) * LANES, LANES), LANES)
        odd = target & 1
        for f in range(FIELDS + 1):
            for j in range(2):
                even_plane = refs[f][2 * j, :, cols].astype(jnp.float32)
                odd_plane = refs[f][2 * j + 1, :, cols].astype(jnp.float32)
                out[part_rows(f, j)] = jnp.where(
                    left,
                    pltpu.roll(even_plane, odd * HALF, 1),
                    pltpu.roll(odd_plane, (1 - odd) * HALF, 1),
                )


    group = iota((OWN, LANES), 1) >> 3

    def plane(x, carry):
        zero = jnp.zeros((OWN, LANES), jnp.float32)
        below, above = [zero] * 5, [zero] * 5
        for f in range(FIELDS + 1):
            in_below, in_above = group == (f + 7) % 16, group == f
            for t in range(2):
                tile = refs[f][x, :, t * LANES : (t + 1) * LANES].astype(jnp.float32)
                near, far = roll(tile, 8 * f, 1), roll(tile, 8 * f - HALF, 1)
                below[2 * t + 1] = jnp.where(in_below, near, below[2 * t + 1])
                below[2 * t + 2] = jnp.where(in_below, far, below[2 * t + 2])
                above[2 * t] = jnp.where(in_above, near, above[2 * t])
                above[2 * t + 1] = jnp.where(in_above, far, above[2 * t + 1])
        for g in range(4):
            edges[g, 0, x] = below[g]
            edges[g, 1, x] = above[g + 1]
        z_up[x] = below[4]
        z_down[x] = above[0]
        return carry

    lax.fori_loop(0, 4, plane, 0)


def edge_kernel(edges, from_below, from_above, own, to1, to2, to3):
    me = position()[0]
    for k, out in enumerate((own, to1, to2, to3)):
        target = me ^ k
        out[0] = jnp.where(target == 0, from_below[...], edges[target, 0])
        out[1] = jnp.where(target == 3, from_above[...], edges[target, 1])


MAIN_TILES = (FIELDS + 1) * 4


def spread_kernel(own, from1, from2, from3, own_z, z1, z2, z3, state, sides, up, down, top):
    me = position()[0]
    peak = jnp.maximum(
        jnp.maximum(own[PART_ROWS:], from1[PART_ROWS:]), jnp.maximum(from2[PART_ROWS:], from3[PART_ROWS:])
    )
    top[...] = jnp.broadcast_to(peak[:1], top.shape)
    for k, (src, side) in enumerate(((own, own_z), (from1, z1), (from2, z2), (from3, z3))):
        block = me ^ k
        for f in range(FIELDS + 1):
            first, second = src[part_rows(f, 0)], src[part_rows(f, 1)]
            state[f, 4 * block] = first
            state[f, 4 * block + 1] = roll(first, HALF, 1)
            state[f, 4 * block + 2] = second
            state[f, 4 * block + 3] = roll(second, HALF, 1)
            up[4 * f + block] = stack_rows(first, second, True)
            down[4 * f + block] = stack_rows(first, second, False)
        for which in range(2):
            for j in range(2):
                even, odd = side[which, 2 * j], side[which, 2 * j + 1]
                sides[which, 4 * block + 2 * j] = even
                sides[which, 4 * block + 2 * j + 1] = odd
                at = MAIN_TILES + 8 * which + 2 * block + j
                up[at] = stack_rows(even, odd, True)
                down[at] = stack_rows(even, odd, False)


def set_masks(width, inside, face_y, face_z):
    _, place_y, chunk, last_y, last_chunk = position()
    shape = (ROWS, LANES)
    row, lane = iota(shape, 0), iota(shape, 1)
    row_ok = (row < OWN) | ((row < OWN + 4) & (place_y < last_y)) | ((row >= OWN + 4) & (place_y > 0))
    lane_ok = (
        (lane < HALF)
        | ((lane < HALF + width) & (chunk < last_chunk))
        | ((lane >= LANES - width) & (chunk > 0))
    )
    ok = jnp.where(row_ok & lane_ok, 1.0, 0.0)
    inside[...] = ok
    face_y[...] = ok * roll(ok, -1, 0)
    face_z[...] = ok * roll(ok, -1, 1)


def step_size(step_no, timestep, tops):
    top_speed = jnp.max(tops[...], axis=0, keepdims=True)
    asked = timestep[step_no]
    return asked / (1.0 + asked * top_speed / cfl_number)


def central(upper, lower):
    return 0.5 * (upper - lower)


def limited(back, fore):
    product = back * fore
    return jnp.where(product > 0.0, product * inverse(back + fore), 0.0)


def carried(positive, here, there, slope_here, slope_there, courant, weight):
    return courant * (
        jnp.where(positive, here, there) + weight * jnp.where(positive, slope_here, slope_there)
    )


def weigh(courant):
    return jnp.where(courant > 0.0, 1.0, -1.0) - courant


def rolled_change(q, positive, courant, weight, axis):
    q_next = roll(q, -1, axis)
    fore = q_next - q
    slope = limited(roll(fore, 1, axis), fore)
    flux = carried(positive, q, q_next, slope, roll(slope, -1, axis), courant, weight)
    return q - (flux - roll(flux, 1, axis))


def rolled_courant(dt, density, momentum, closed, axis):
    velocity = momentum * inverse(density)
    return dt * 0.5 * (velocity + roll(velocity, -1, axis)) * closed


def strain_pass(dt, state, stress, rest, inside):
    def strain_plane(p, carry):
        at = p + PAD
        ok = inside[...] > 0.0
        vel = [state[2 + i, at] for i in range(3)]
        grad = [
            [
                central(state[2 + i, at + 1], state[2 + i, at - 1]),
                central(roll(vel[i], -1, 0), roll(vel[i], 1, 0)),
                central(roll(vel[i], -1, 1), roll(vel[i], 1, 1)),
            ]
            for i in range(3)
        ]
        third_div = (grad[0][0] + grad[1][1] + grad[2][2]) * (1.0 / 3.0)
        strain = [
            grad[0][0] - third_div,
            grad[1][1] - third_div,
            grad[2][2] - third_div,
            0.5 * (grad[0][1] + grad[1][0]),
            0.5 * (grad[1][2] + grad[2][1]),
            0.5 * (grad[0][2] + grad[2][0]),
        ]
        kind = state[FIELDS, at]
        first, second = kind == 0.0, kind == 1.0
        density, energy = state[0, at], state[1, at]
        plastic, damage = state[5, at], state[6, at]
        pressure = (
            pick(first, second, tuple(c * c for c in sound_table))
            * (density - pick(first, second, rest_table))
            + pick(first, second, gruneisen_table) * density * energy
        )
        shear_dt = pick(first, second, tuple(2.0 * g for g in shear_table)) * dt
        trial = [state[7 + k, at] + shear_dt * strain[k] for k in range(6)]
        trial_sq = (
            trial[0] * trial[0]
            + trial[1] * trial[1]
            + trial[2] * trial[2]
            + 2.0 * (trial[3] * trial[3] + trial[4] * trial[4] + trial[5] * trial[5])
        )
        strain_sq = (
            strain[0] * strain[0]
            + strain[1] * strain[1]
            + strain[2] * strain[2]
            + 2.0 * (strain[3] * strain[3] + strain[4] * strain[4] + strain[5] * strain[5])
        )
        equivalent = jnp.sqrt(1.5 * trial_sq)
        strain_rate = jnp.sqrt(strain_sq * (2.0 / 3.0))
        hardened = pick(first, second, yield_table) + pick(first, second, harden_table) * jnp.exp(
            pick(first, second, exponent_table) * jnp.log(plastic)
        )
        flow = (
            hardened
            * (1.0 + pick(first, second, rate_table) * jnp.log(1.0 + strain_rate))
            * (1.0 - damage)
        )
        bound = jnp.maximum(equivalent, flow)
        per_bound = inverse(bound)
        factor = flow * per_bound
        increment = (bound - flow) * pick(first, second, tuple(1.0 / (3.0 * g) for g in shear_table))
        triaxial = jnp.clip(-pressure * per_bound, -1.5, 1.5)
        failure = 0.05 + 0.8 * jnp.exp(-1.5 * triaxial)
        rest[1, p] = jnp.where(ok, density * (plastic + increment), 0.0)
        worn = jnp.minimum(damage + increment * inverse(failure), 0.9)
        rest[2, p] = jnp.where(ok, density * worn, 0.0)
        dev = [jnp.where(ok, trial[k] * factor, 0.0) for k in range(6)]
        held = jnp.where(ok, pressure, 0.0)
        full = [dev[0] - held, dev[1] - held, dev[2] - held, dev[3], dev[4], dev[5]]
        for k in range(6):
            rest[3 + k, p] = density * dev[k]
            stress[k, p + 1] = full[k]
        work = (
            full[0] * grad[0][0]
            + full[1] * grad[1][1]
            + full[2] * grad[2][2]
            + 2.0 * (full[3] * strain[3] + full[4] * strain[4] + full[5] * strain[5])
        )
        rest[0, p] = jnp.where(ok, density * energy + dt * work, 0.0)
        return carry

    zero = jnp.zeros((ROWS, LANES), jnp.float32)
    for k in range(6):
        stress[k, 0] = zero
        stress[k, PLANES + 1] = zero
    lax.fori_loop(0, PLANES, strain_plane, 0)


def force_pass(dt, state, stress, lead, inside):
    def force_plane(p, carry):
        at = p + PAD
        density = state[0, at]
        here = [stress[k, p + 1] for k in range(6)]
        lead[0, p] = density
        for i in range(3):
            along_x, along_y, along_z = ACROSS[0][i], ACROSS[1][i], ACROSS[2][i]
            force = (
                central(stress[along_x, p + 2], stress[along_x, p])
                + central(roll(here[along_y], -1, 0), roll(here[along_y], 1, 0))
                + central(roll(here[along_z], -1, 1), roll(here[along_z], 1, 1))
            )
            lead[1 + i, p] = density * state[2 + i, at] + jnp.where(inside[...] > 0.0, dt * force, 0.0)
        return carry

    lax.fori_loop(0, PLANES, force_plane, 0)


def first_sweep(fields, moved, courants):
    def field(f, carry):
        here = fields[f, 0]
        ahead = fields[f, 1]
        fore = ahead - here
        slope = limited(here, fore)
        last_flux = None
        for p in range(PLANES - 1):
            further = fields[f, p + 2] if p + 2 < PLANES else 0.0
            next_fore = further - ahead
            next_slope = limited(fore, next_fore)
            courant = courants[p]
            flux = carried(courant > 0.0, here, ahead, slope, next_slope, courant, weigh(courant))
            moved[f, p] = here - (flux if last_flux is None else flux - last_flux)
            last_flux, here, ahead, fore, slope = flux, ahead, further, next_fore, next_slope
        moved[f, PLANES - 1] = here + last_flux
        return carry

    lax.fori_loop(0, fields.shape[0], field, 0)


def first_courants(dt, lead, courants, inside):
    ok = inside[...] > 0.0
    here = None
    for p in range(PLANES):
        ahead = lead[1, p] * inverse(jnp.where(ok, lead[0, p], 1.0))
        if p > 0:
            courants[p - 1] = dt * 0.5 * (here + ahead)
        here = ahead


def later_sweeps(count, moved, mids, second_courant, third_courant, finish):
    def second(p, mid):
        courant = second_courant(p)
        positive, weight = courant > 0.0, weigh(courant)
        for f in range(count):
            mid[f] = rolled_change(moved[f, p], positive, courant, weight, 0)[:OWN]
            yield

    def third(p, mid):
        courant = third_courant(p, mid)
        positive, weight = courant > 0.0, weigh(courant)
        scale = None
        for f in range(count):
            value = rolled_change(mid[f], positive, courant, weight, 1)
            scale = finish(p, f, value, scale)
            yield

    def beside(*parts):
        for _ in zip(*parts):
            pass

    def pair(i, carry):
        beside(second(2 * i + 1, mids.at[1]), third(2 * i, mids.at[0]))
        beside(second(jnp.minimum(2 * i + 2, PLANES - 1), mids.at[0]), third(2 * i + 1, mids.at[1]))
        return carry

    beside(second(0, mids.at[0]))
    lax.fori_loop(0, PLANES // 2, pair, 0)


LEAD = 4
REST = 9
LEAD_AT = (0, 2, 3, 4)
REST_AT = (1, 5, 6, 7, 8, 9, 10, 11, 12)


def sweep_lead(dt, lead, moved, mids, courants, scales, inside, face_y, face_z, put):
    along_x, along_y, along_z = courants
    first_courants(dt, lead, along_x, inside)
    first_sweep(lead, moved, along_x)

    def second_courant(p):
        density = jnp.where(inside[...] > 0.0, moved[0, p], 1.0)
        courant = rolled_courant(dt, density, moved[2, p], face_y[...], 0)
        along_y[p] = courant
        return courant

    def third_courant(p, mid):
        density = jnp.where(inside[:OWN] > 0.0, mid[0], 1.0)
        courant = rolled_courant(dt, density, mid[3], face_z[:OWN], 1)
        along_z[p] = courant
        return courant

    def finish(p, f, value, scale):
        if f == 0:
            ok = inside[:OWN] > 0.0
            scale = jnp.where(ok, inverse(jnp.where(ok, value, 1.0)), 0.0)
            scales[p] = scale
            put(0, p, jnp.where(ok, value, 0.0))
        else:
            put(f, p, value * scale)
        return scale

    later_sweeps(LEAD, moved, mids, second_courant, third_courant, finish)


def sweep_rest(rest, moved, mids, courants, scales, put):
    along_x, along_y, along_z = courants
    first_sweep(rest, moved, along_x)

    def finish(p, f, value, scale):
        put(f, p, value * scales[p])

    later_sweeps(REST, moved, mids, lambda p: along_y[p], lambda p, mid: along_z[p], finish)


def clear_ends(state):
    zero = jnp.zeros((ROWS, LANES), jnp.float32)
    for f in range(FIELDS + 1):
        for p in (0, 1, PLANES + PAD, PLANES + PAD + 1):
            state[f, p] = zero


def lead_kernel(
    timestep, tops, own, sides, low, high, out, rest, along_x, along_y, along_z, scales, kinds, top,
    state, stress, lead, moved, mids, inside, face_y, face_z,
):
    set_masks(8, inside, face_y, face_z)
    clear_ends(state)
    dt = step_size(0, timestep, tops)

    def gather(block, carry):
        ok = inside[...] > 0.0
        lane = iota((ROWS, LANES), 1)
        group = lane >> 3
        for j in range(2):
            around = []
            for odd in range(2):
                p = 4 * block + 2 * j + odd
                for which in range(2):
                    at = MAIN_TILES + 8 * which + 2 * block + j
                    tile = halo_tile(high[at], low[at], odd == 1)
                    around.append(jnp.concatenate([sides[which, p], tile], axis=0))
            for f in range(FIELDS + 1):
                tile = halo_tile(high[4 * f + block], low[4 * f + block], j == 1)
                for odd in range(2):
                    p = 4 * block + 2 * j + odd
                    below, above = around[2 * odd], around[2 * odd + 1]
                    value = jnp.concatenate([own[f, p], roll(tile, HALF * odd, 1)], axis=0)
                    side = roll(jnp.where(group == f, above, below), HALF - 8 * f, 1)
                    value = jnp.where(ok, jnp.where(lane < HALF, value, side), 0.0)
                    state[f, p + PAD] = value
                    if f == FIELDS:
                        kinds[p] = value
        return carry

    lax.fori_loop(0, 4, gather, 0)
    strain_pass(dt, state, stress, rest, inside)
    force_pass(dt, state, stress, lead, inside)

    def put(f, p, value):
        out[f, p] = value

    sweep_lead(
        dt, lead, moved, mids, (along_x, along_y, along_z), scales, inside, face_y, face_z, put
    )

    def peaks(p, peak):
        speed = jnp.maximum(jnp.abs(out[1, p]), jnp.abs(out[2, p]))
        speed = jnp.maximum(speed, jnp.abs(out[3, p]))
        kind = kinds[p, :OWN]
        speed = speed + pick(kind == 0.0, kind == 1.0, sound_table)
        lane = iota((OWN, LANES), 1)
        return jnp.maximum(peak, jnp.where(lane < HALF, speed, 0.0))

    peak = lax.fori_loop(0, PLANES, peaks, jnp.zeros((OWN, LANES), jnp.float32))
    top[...] = jnp.full(top.shape, jnp.max(peak), jnp.float32)


def rest_kernel(lead, rest, along_x, along_y, along_z, scales, out, up, down, moved, mids):
    def put(f, p, value):
        out[f, p] = value

    sweep_rest(rest, moved, mids, (along_x, along_y, along_z), scales, put)

    def messages(i, carry):
        for f in range(FIELDS):
            src, at = (lead, LEAD_AT.index(f)) if f in LEAD_AT else (out, REST_AT.index(f))
            even, odd = src[at, 2 * i], src[at, 2 * i + 1]
            up[f, i] = stack_rows(even, odd, True)
            down[f, i] = stack_rows(even, odd, False)
        return carry

    lax.fori_loop(0, PLANES // 2, messages, 0)


def second_kernel(
    timestep, tops, own_lead, own_rest, kinds, low, high, mine, to1, to2, to3,
    state, stress, lead, moved, mids, inside, face_y, face_z,
    rest, rest_moved, rest_mids, along_x, along_y, along_z, scales, out,
):
    set_masks(4, inside, face_y, face_z)
    clear_ends(state)
    dt = step_size(1, timestep, tops)

    def gather(i, carry):
        ok = inside[...] > 0.0
        for f in range(FIELDS):
            src, at = (own_lead, LEAD_AT.index(f)) if f in LEAD_AT else (own_rest, REST_AT.index(f))
            for odd in range(2):
                p = 2 * i + odd
                tile = halo_tile(high[f, i], low[f, i], odd == 1)
                value = jnp.concatenate([src[at, p], tile], axis=0)
                state[f, p + PAD] = jnp.where(ok, value, 0.0)
        for odd in range(2):
            state[FIELDS, 2 * i + odd + PAD] = kinds[2 * i + odd]
        return carry

    lax.fori_loop(0, PLANES // 2, gather, 0)
    strain_pass(dt, state, stress, rest, inside)
    force_pass(dt, state, stress, lead, inside)
    courants = (along_x, along_y, along_z)

    def put_lead(f, p, value):
        out[LEAD_AT[f], p] = value

    def put_rest(f, p, value):
        out[REST_AT[f], p] = value

    sweep_lead(dt, lead, moved, mids, courants, scales, inside, face_y, face_z, put_lead)
    sweep_rest(rest, rest_moved, rest_mids, courants, scales, put_rest)

    left = iota((OWN, LANES), 1) < HALF
    for k, dest in enumerate((mine, to1, to2, to3)):
        block = position()[0] ^ k
        for f in range(FIELDS):
            for j in range(2):
                even, odd = out[f, 4 * block + 2 * j], out[f, 4 * block + 2 * j + 1]
                dest[f, j] = jnp.where(left, even, roll(odd, HALF, 1))


def unpack_kernel(mine, from1, from2, from3, dens, ener, vel, plas, dama, devi, held):
    me = position()[0]
    refs = [dens, ener] + [vel.at[i] for i in range(3)] + [plas, dama]
    refs = refs + [devi.at[i] for i in range(6)]
    for k, src in enumerate((mine, from1, from2, from3)):
        held[me ^ k] = src[...]
    left = iota((OWN, LANES), 1) < HALF
    for f in range(FIELDS):
        for j in range(2):
            for t in range(2):
                first, second = held[2 * t, f, j], held[2 * t + 1, f, j]
                cols = slice(t * LANES, (t + 1) * LANES)
                refs[f][2 * j, :, cols] = jnp.where(left, first, roll(second, HALF, 1))
                refs[f][2 * j + 1, :, cols] = jnp.where(left, roll(first, HALF, 1), second)


IN_VMEM = pl.BlockSpec(memory_space=pltpu.VMEM)
IN_SMEM = pl.BlockSpec(memory_space=pltpu.SMEM)


def call(kernel, scalars, outs, scratch, *args):
    return pl.pallas_call(
        kernel,
        out_shape=[jax.ShapeDtypeStruct(shape, jnp.float32) for shape in outs],
        in_specs=[IN_SMEM] * scalars + [IN_VMEM] * (len(args) - scalars),
        out_specs=[IN_VMEM] * len(outs),
        scratch_shapes=[pltpu.VMEM(shape, jnp.float32) for shape in scratch],
        compiler_params=pltpu.CompilerParams(vmem_limit_bytes=48 * 1024 * 1024),
    )(*args)


def ring_pair(to_next, to_last, axes, order):
    after = order[1:] + order[:1]
    low = lax.ppermute(to_next, axes, list(zip(order, after)))
    high = lax.ppermute(to_last, axes, list(zip(after, order)))
    return low, high


def swap_blocks(parts):
    count = lax.axis_size("gx")
    return [
        lax.ppermute(part, "gx", [(i, i ^ (k + 1)) for i in range(count)])
        for k, part in enumerate(parts)
    ]


def shards(density, energy, velocity, plastic_strain, damage, deviator, materials, timestep):
    size_y, size_z = lax.axis_size("gy"), lax.axis_size("gz")
    all_fields = FIELDS + 1
    part = (PART_ROWS + 8, LANES)
    inputs = (density, energy, velocity, plastic_strain, damage, deviator, materials)
    edge = (4, OWN, LANES)
    own, *parts, edges, z_up, z_down = pl.pallas_call(
        pack_kernel,
        out_shape=[
            jax.ShapeDtypeStruct(shape, jnp.float32) for shape in [part] * 4 + [(4, 2) + edge, edge, edge]
        ],
        in_specs=[pl.BlockSpec(memory_space=pltpu.HBM)] * len(inputs),
        out_specs=[IN_VMEM] * 7,
        scratch_shapes=[pltpu.VMEM(array.shape, array.dtype) for array in inputs]
        + [pltpu.SemaphoreType.DMA((len(inputs),))],
        compiler_params=pltpu.CompilerParams(vmem_limit_bytes=PACK_LIMIT),
    )(*inputs)
    z_low, z_high = ring_pair(z_up, z_down, "gz", list(range(size_z)))
    parts = swap_blocks(parts)
    own_z, *z_parts = call(edge_kernel, 0, [(2,) + edge] * 4, [], edges, z_low, z_high)
    z_parts = swap_blocks(z_parts)
    message = (MAIN_TILES + PLANES, 8, LANES)
    state, sides, up, down, top = call(
        spread_kernel,
        0,
        [(all_fields, PLANES, OWN, LANES), (2, PLANES, OWN, LANES), message, message]
        + [(size_y * size_z, LANES)],
        [],
        own,
        *parts,
        own_z,
        *z_parts,
    )
    low, high = ring_pair(up, down, "gy", list(range(size_y)))
    tops = lax.all_to_all(top, ("gy", "gz"), 0, 0)
    full = (ROWS, LANES)
    scratch = [
        (all_fields, PLANES + 2 * PAD) + full,
        (6, PLANES + 2) + full,
        (LEAD, PLANES) + full,
        (LEAD, PLANES) + full,
        (2, LEAD, OWN, LANES),
        full,
        full,
        full,
    ]
    left_over = [
        (REST, PLANES) + full,
        (PLANES - 1,) + full,
        (PLANES,) + full,
        (PLANES, OWN, LANES),
        (PLANES, OWN, LANES),
    ]
    rest_scratch = [(REST, PLANES) + full, (2, REST, OWN, LANES)]
    lead, *rest, kinds, top = call(
        lead_kernel,
        1,
        [(LEAD, PLANES, OWN, LANES)] + left_over + [(PLANES,) + full, (8, LANES)],
        scratch,
        timestep,
        tops,
        state,
        sides,
        low,
        high,
    )
    others = swap_blocks([top] * 3)
    rest, up, down = call(
        rest_kernel,
        0,
        [(REST, PLANES, OWN, LANES)] + [(FIELDS, PLANES // 2, 8, LANES)] * 2,
        rest_scratch,
        lead,
        *rest,
    )
    low, high = ring_pair(up, down, "gy", list(range(size_y)))
    for other in others:
        top = jnp.maximum(top, other)
    tops = lax.all_to_all(jnp.broadcast_to(top[:1], (size_y * size_z, LANES)), ("gy", "gz"), 0, 0)
    mine, *parts = call(
        second_kernel,
        1,
        [(FIELDS, 2, OWN, LANES)] * 4,
        scratch + left_over[:1] + rest_scratch + left_over[1:] + [(FIELDS, PLANES, OWN, LANES)],
        timestep,
        tops,
        lead,
        rest,
        kinds,
        low,
        high,
    )
    parts = swap_blocks(parts)
    cells = density.shape
    return tuple(
        call(
            unpack_kernel,
            0,
            [cells, cells, (3,) + cells, cells, cells, (6,) + cells],
            [(4, FIELDS, 2, OWN, LANES)],
            mine,
            *parts,
        )
    )


def solution(mesh):
    cells = P("gx", "gy", "gz")
    vectors = P(None, "gx", "gy", "gz")
    return jax.shard_map(
        shards,
        mesh=mesh,
        in_specs=(cells, cells, vectors, cells, cells, vectors, cells, P()),
        out_specs=(cells, cells, vectors, cells, cells, vectors),
        check_vma=False,
    )
```

```python
import jax
import jax.numpy as jnp
from jax import lax
from jax.experimental import pallas as pl
from jax.experimental.pallas import tpu as pltpu
from jax.sharding import PartitionSpec as P


FIELDS = 13
PLANES = 16
ROWS = 24
OWN = 16
LANES = 128
HALF = 64
DEPTH = 80
GROUP = 8
PAD = 2

shear_table = (1.0, 0.5, 0.8)
sound_table = (1.5, 1.2, 1.0)
gruneisen_table = (2.0, 2.1, 1.9)
rest_table = (4.0, 3.0, 5.0)
yield_table = (0.3, 0.2, 0.25)
harden_table = (0.5, 0.3, 0.4)
exponent_table = (0.3, 0.4, 0.35)
rate_table = (0.02, 0.015, 0.01)
cfl_number = 0.2

PACK_LIMIT = 62 * 1024 * 1024
ACROSS = ((0, 3, 5), (3, 1, 4), (5, 4, 2))


def roll(value, shift, axis):
    shift = shift % value.shape[axis]
    return value if shift == 0 else pltpu.roll(value, shift, axis)


def position():
    size_x = lax.axis_size("gx")
    place_x = lax.axis_index("gx")
    chunk = lax.axis_index("gz") * size_x + place_x
    return place_x, lax.axis_index("gy"), chunk, lax.axis_size("gy") - 1, size_x * lax.axis_size("gz") - 1


def iota(shape, axis):
    return lax.broadcasted_iota(jnp.int32, shape, axis)


def inverse(value):
    guess = pl.reciprocal(value, approx=True)
    return guess * (2.0 - value * guess)


def pick(first, second, table):
    return jnp.where(first, table[0], jnp.where(second, table[1], table[2]))


def stack_rows(even, odd, upper):
    low_rows = iota((8, LANES), 0) < 4
    if upper:
        return jnp.where(low_rows, roll(even[8:], 4, 0), odd[8:])
    return jnp.where(low_rows, even[:8], roll(odd[:8], 4, 0))


def halo_tile(high, low, odd):
    low_rows = iota((8, LANES), 0) < 4
    if odd:
        return jnp.where(low_rows, roll(high, 4, 0), low)
    return jnp.where(low_rows, high, roll(low, 4, 0))


PART_ROWS = (FIELDS + 1) * 2 * OWN


def part_rows(f, j):
    return slice((2 * f + j) * OWN, (2 * f + j + 1) * OWN)


def pack_kernel(*args):
    sources, (own, to1, to2, to3, edges, z_up, z_down) = args[:7], args[7:14]
    buffers, arrived = args[14:21], args[21]
    copies = [
        pltpu.make_async_copy(source, buffer, arrived.at[i])
        for i, (source, buffer) in enumerate(zip(sources, buffers))
    ]
    for copy in copies:
        copy.start()
    for copy in copies:
        copy.wait()
    dens, ener, vel, plas, dama, devi, mat = buffers
    me = position()[0]
    refs = [dens, ener] + [vel.at[i] for i in range(3)] + [plas, dama]
    refs = refs + [devi.at[i] for i in range(6)] + [mat]
    peak = None
    for x in range(4):
        for t in range(2):
            cols = slice(t * LANES, (t + 1) * LANES)
            speed = jnp.maximum(jnp.abs(vel[0, x, :, cols]), jnp.abs(vel[1, x, :, cols]))
            speed = jnp.maximum(speed, jnp.abs(vel[2, x, :, cols]))
            kind = mat[x, :, cols]
            speed = speed + pick(kind == 0, kind == 1, sound_table)
            peak = speed if peak is None else jnp.maximum(peak, speed)
    peak = jnp.full((8, LANES), jnp.max(peak), jnp.float32)
    left = iota((OWN, LANES), 1) < HALF
    for k, out in enumerate((own, to1, to2, to3)):
        out[PART_ROWS:] = peak
        target = me ^ k
        cols = pl.ds(pl.multiple_of((target >> 1) * LANES, LANES), LANES)
        odd = target & 1
        for f in range(FIELDS + 1):
            for j in range(2):
                even_plane = refs[f][2 * j, :, cols].astype(jnp.float32)
                odd_plane = refs[f][2 * j + 1, :, cols].astype(jnp.float32)
                out[part_rows(f, j)] = jnp.where(
                    left,
                    pltpu.roll(even_plane, odd * HALF, 1),
                    pltpu.roll(odd_plane, (1 - odd) * HALF, 1),
                )


    group = iota((OWN, LANES), 1) >> 3

    def plane(x, carry):
        zero = jnp.zeros((OWN, LANES), jnp.float32)
        below, above = [zero] * 5, [zero] * 5
        for f in range(FIELDS + 1):
            in_below, in_above = group == (f + 7) % 16, group == f
            for t in range(2):
                tile = refs[f][x, :, t * LANES : (t + 1) * LANES].astype(jnp.float32)
                near, far = roll(tile, 8 * f, 1), roll(tile, 8 * f - HALF, 1)
                below[2 * t + 1] = jnp.where(in_below, near, below[2 * t + 1])
                below[2 * t + 2] = jnp.where(in_below, far, below[2 * t + 2])
                above[2 * t] = jnp.where(in_above, near, above[2 * t])
                above[2 * t + 1] = jnp.where(in_above, far, above[2 * t + 1])
        for g in range(4):
            edges[g, 0, x] = below[g]
            edges[g, 1, x] = above[g + 1]
        z_up[x] = below[4]
        z_down[x] = above[0]
        return carry

    lax.fori_loop(0, 4, plane, 0)


def edge_kernel(edges, from_below, from_above, own, to1, to2, to3):
    me = position()[0]
    for k, out in enumerate((own, to1, to2, to3)):
        target = me ^ k
        out[0] = jnp.where(target == 0, from_below[...], edges[target, 0])
        out[1] = jnp.where(target == 3, from_above[...], edges[target, 1])


MAIN_TILES = (FIELDS + 1) * 4


def spread_kernel(own, from1, from2, from3, own_z, z1, z2, z3, state, sides, up, down, top):
    me = position()[0]
    peak = jnp.maximum(
        jnp.maximum(own[PART_ROWS:], from1[PART_ROWS:]), jnp.maximum(from2[PART_ROWS:], from3[PART_ROWS:])
    )
    top[...] = jnp.broadcast_to(peak[:1], top.shape)
    for k, (src, side) in enumerate(((own, own_z), (from1, z1), (from2, z2), (from3, z3))):
        block = me ^ k
        for f in range(FIELDS + 1):
            first, second = src[part_rows(f, 0)], src[part_rows(f, 1)]
            state[f, 4 * block] = first
            state[f, 4 * block + 1] = roll(first, HALF, 1)
            state[f, 4 * block + 2] = second
            state[f, 4 * block + 3] = roll(second, HALF, 1)
            up[4 * f + block] = stack_rows(first, second, True)
            down[4 * f + block] = stack_rows(first, second, False)
        for which in range(2):
            for j in range(2):
                even, odd = side[which, 2 * j], side[which, 2 * j + 1]
                sides[which, 4 * block + 2 * j] = even
                sides[which, 4 * block + 2 * j + 1] = odd
                at = MAIN_TILES + 8 * which + 2 * block + j
                up[at] = stack_rows(even, odd, True)
                down[at] = stack_rows(even, odd, False)


def set_masks(width, inside, face_y, face_z):
    _, place_y, chunk, last_y, last_chunk = position()
    shape = (ROWS, LANES)
    row, lane = iota(shape, 0), iota(shape, 1)
    row_ok = (row < OWN) | ((row < OWN + 4) & (place_y < last_y)) | ((row >= OWN + 4) & (place_y > 0))
    lane_ok = (
        (lane < HALF)
        | ((lane < HALF + width) & (chunk < last_chunk))
        | ((lane >= LANES - width) & (chunk > 0))
    )
    ok = jnp.where(row_ok & lane_ok, 1.0, 0.0)
    inside[...] = ok
    face_y[...] = ok * roll(ok, -1, 0)
    row = iota((DEPTH, LANES), 0)
    row_ok = (
        (row < HALF)
        | ((row < HALF + width) & (chunk < last_chunk))
        | ((row >= DEPTH - width) & (chunk > 0))
    )
    ok = jnp.where(row_ok, 1.0, 0.0)
    face_z[0] = ok
    face_z[1] = ok * roll(ok, -1, 0)


def step_size(step_no, timestep, tops):
    top_speed = jnp.max(tops[...], axis=0, keepdims=True)
    asked = timestep[step_no]
    return asked / (1.0 + asked * top_speed / cfl_number)


def central(upper, lower):
    return 0.5 * (upper - lower)


def limited(back, fore):
    product = back * fore
    return jnp.where(product > 0.0, product * inverse(back + fore), 0.0)


def carried(positive, here, there, slope_here, slope_there, courant, weight):
    return courant * (
        jnp.where(positive, here, there) + weight * jnp.where(positive, slope_here, slope_there)
    )


def weigh(courant):
    return jnp.where(courant > 0.0, 1.0, -1.0) - courant


def rolled_change(q, positive, courant, weight):
    q_next = roll(q, -1, 0)
    fore = q_next - q
    slope = limited(roll(fore, 1, 0), fore)
    flux = carried(positive, q, q_next, slope, roll(slope, -1, 0), courant, weight)
    return q - (flux - roll(flux, 1, 0))


def rolled_courant(dt, density, momentum, closed):
    velocity = momentum * inverse(density)
    return dt * 0.5 * (velocity + roll(velocity, -1, 0)) * closed


def strain_pass(dt, state, stress, rest, inside):
    def strain_plane(p, carry):
        at = p + PAD
        ok = inside[...] > 0.0
        vel = [state[2 + i, at] for i in range(3)]
        grad = [
            [
                central(state[2 + i, at + 1], state[2 + i, at - 1]),
                central(roll(vel[i], -1, 0), roll(vel[i], 1, 0)),
                central(roll(vel[i], -1, 1), roll(vel[i], 1, 1)),
            ]
            for i in range(3)
        ]
        third_div = (grad[0][0] + grad[1][1] + grad[2][2]) * (1.0 / 3.0)
        strain = [
            grad[0][0] - third_div,
            grad[1][1] - third_div,
            grad[2][2] - third_div,
            0.5 * (grad[0][1] + grad[1][0]),
            0.5 * (grad[1][2] + grad[2][1]),
            0.5 * (grad[0][2] + grad[2][0]),
        ]
        kind = state[FIELDS, at]
        first, second = kind == 0.0, kind == 1.0
        density, energy = state[0, at], state[1, at]
        plastic, damage = state[5, at], state[6, at]
        pressure = (
            pick(first, second, tuple(c * c for c in sound_table))
            * (density - pick(first, second, rest_table))
            + pick(first, second, gruneisen_table) * density * energy
        )
        shear_dt = pick(first, second, tuple(2.0 * g for g in shear_table)) * dt
        trial = [state[7 + k, at] + shear_dt * strain[k] for k in range(6)]
        trial_sq = (
            trial[0] * trial[0]
            + trial[1] * trial[1]
            + trial[2] * trial[2]
            + 2.0 * (trial[3] * trial[3] + trial[4] * trial[4] + trial[5] * trial[5])
        )
        strain_sq = (
            strain[0] * strain[0]
            + strain[1] * strain[1]
            + strain[2] * strain[2]
            + 2.0 * (strain[3] * strain[3] + strain[4] * strain[4] + strain[5] * strain[5])
        )
        equivalent = jnp.sqrt(1.5 * trial_sq)
        strain_rate = jnp.sqrt(strain_sq * (2.0 / 3.0))
        hardened = pick(first, second, yield_table) + pick(first, second, harden_table) * jnp.exp(
            pick(first, second, exponent_table) * jnp.log(plastic)
        )
        flow = (
            hardened
            * (1.0 + pick(first, second, rate_table) * jnp.log(1.0 + strain_rate))
            * (1.0 - damage)
        )
        bound = jnp.maximum(equivalent, flow)
        per_bound = inverse(bound)
        factor = flow * per_bound
        increment = (bound - flow) * pick(first, second, tuple(1.0 / (3.0 * g) for g in shear_table))
        triaxial = jnp.clip(-pressure * per_bound, -1.5, 1.5)
        failure = 0.05 + 0.8 * jnp.exp(-1.5 * triaxial)
        rest[1, p] = jnp.where(ok, density * (plastic + increment), 0.0)
        worn = jnp.minimum(damage + increment * inverse(failure), 0.9)
        rest[2, p] = jnp.where(ok, density * worn, 0.0)
        dev = [jnp.where(ok, trial[k] * factor, 0.0) for k in range(6)]
        held = jnp.where(ok, pressure, 0.0)
        full = [dev[0] - held, dev[1] - held, dev[2] - held, dev[3], dev[4], dev[5]]
        for k in range(6):
            rest[3 + k, p] = density * dev[k]
            stress[k, p + 1] = full[k]
        work = (
            full[0] * grad[0][0]
            + full[1] * grad[1][1]
            + full[2] * grad[2][2]
            + 2.0 * (full[3] * strain[3] + full[4] * strain[4] + full[5] * strain[5])
        )
        rest[0, p] = jnp.where(ok, density * energy + dt * work, 0.0)
        return carry

    zero = jnp.zeros((ROWS, LANES), jnp.float32)
    for k in range(6):
        stress[k, 0] = zero
        stress[k, PLANES + 1] = zero
    lax.fori_loop(0, PLANES, strain_plane, 0)


def force_pass(dt, state, stress, lead, inside):
    def force_plane(p, carry):
        at = p + PAD
        density = state[0, at]
        here = [stress[k, p + 1] for k in range(6)]
        lead[0, p] = density
        for i in range(3):
            along_x, along_y, along_z = ACROSS[0][i], ACROSS[1][i], ACROSS[2][i]
            force = (
                central(stress[along_x, p + 2], stress[along_x, p])
                + central(roll(here[along_y], -1, 0), roll(here[along_y], 1, 0))
                + central(roll(here[along_z], -1, 1), roll(here[along_z], 1, 1))
            )
            lead[1 + i, p] = density * state[2 + i, at] + jnp.where(inside[...] > 0.0, dt * force, 0.0)
        return carry

    lax.fori_loop(0, PLANES, force_plane, 0)


def first_sweep(fields, moved, courants):
    def field(f, carry):
        here = fields[f, 0]
        ahead = fields[f, 1]
        fore = ahead - here
        slope = limited(here, fore)
        last_flux = None
        for p in range(PLANES - 1):
            further = fields[f, p + 2] if p + 2 < PLANES else 0.0
            next_fore = further - ahead
            next_slope = limited(fore, next_fore)
            courant = courants[p]
            flux = carried(courant > 0.0, here, ahead, slope, next_slope, courant, weigh(courant))
            moved[f, p] = here - (flux if last_flux is None else flux - last_flux)
            last_flux, here, ahead, fore, slope = flux, ahead, further, next_fore, next_slope
        moved[f, PLANES - 1] = here + last_flux
        return carry

    lax.fori_loop(0, fields.shape[0], field, 0)


def first_courants(dt, lead, courants, inside):
    ok = inside[...] > 0.0
    here = None
    for p in range(PLANES):
        ahead = lead[1, p] * inverse(jnp.where(ok, lead[0, p], 1.0))
        if p > 0:
            courants[p - 1] = dt * 0.5 * (here + ahead)
        here = ahead


def second_sweep(moved, f, group, courant_of, mid):
    for i in range(GROUP):
        p = GROUP * group + i
        courant = courant_of(p)
        value = rolled_change(moved[f, p], courant > 0.0, courant, weigh(courant))
        mid[OWN * i : OWN * (i + 1)] = value[:OWN]


def turned(mid):
    value = mid[...].T
    return jnp.concatenate([value[: HALF + 8], value[LANES - 8 :]], axis=0)


def turn_back(value, put, f, group):
    gap = jnp.zeros((LANES - DEPTH, LANES), jnp.float32)
    value = jnp.concatenate([value[: HALF + 8], gap, value[HALF + 8 :]], axis=0).T
    for i in range(GROUP):
        put(f, GROUP * group + i, value[OWN * i : OWN * (i + 1)])


LEAD = 4
REST = 9
LEAD_AT = (0, 2, 3, 4)
REST_AT = (1, 5, 6, 7, 8, 9, 10, 11, 12)
ORDER = tuple((LEAD_AT + REST_AT).index(f) for f in range(FIELDS))


def sweep_lead(dt, lead, moved, mids, courants, scales, inside, face_y, face_z, put):
    along_x, along_y, along_z = courants
    first_courants(dt, lead, along_x, inside)
    first_sweep(lead, moved, along_x)

    def second_courant(p):
        density = jnp.where(inside[...] > 0.0, moved[0, p], 1.0)
        courant = rolled_courant(dt, density, moved[2, p], face_y[...])
        along_y[p] = courant
        return courant

    def second(group):
        second_sweep(moved, 0, group, second_courant, mids.at[group, 0])
        for f in range(1, LEAD):
            second_sweep(moved, f, group, lambda p: along_y[p], mids.at[group, f])

    def third(group):
        ok = face_z[0] > 0.0
        density = turned(mids.at[group, 0])
        momentum = turned(mids.at[group, 3])
        courant = rolled_courant(dt, jnp.where(ok, density, 1.0), momentum, face_z[1])
        along_z[group] = courant
        positive, weight = courant > 0.0, weigh(courant)
        value = rolled_change(density, positive, courant, weight)
        scale = jnp.where(ok, inverse(jnp.where(ok, value, 1.0)), 0.0)
        scales[group] = scale
        turn_back(jnp.where(ok, value, 0.0), put, 0, group)
        for f in range(1, LEAD):
            value = turned(mids.at[group, f]) if f < 3 else momentum
            turn_back(rolled_change(value, positive, courant, weight) * scale, put, f, group)

    second(0)
    second(1)
    third(0)
    third(1)


def sweep_rest(rest, moved, mids, courants, scales, put):
    along_x, along_y, along_z = courants
    first_sweep(rest, moved, along_x)

    def field(f, carry):
        for group in range(2):
            courant = along_z[group]
            value = rolled_change(turned(mids.at[group]), courant > 0.0, courant, weigh(courant))
            turn_back(value * scales[group], put, f, group)
            second_sweep(moved, jnp.minimum(f + 1, REST - 1), group, lambda p: along_y[p], mids.at[group])
        return carry

    for group in range(2):
        second_sweep(moved, 0, group, lambda p: along_y[p], mids.at[group])
    lax.fori_loop(0, REST, field, 0)


def clear_ends(state):
    zero = jnp.zeros((ROWS, LANES), jnp.float32)
    for f in range(FIELDS + 1):
        for p in (0, 1, PLANES + PAD, PLANES + PAD + 1):
            state[f, p] = zero


def lead_kernel(
    timestep, tops, own, sides, low, high, out, rest, along_x, along_y, along_z, scales, kinds, top,
    state, stress, lead, moved, mids, inside, face_y, face_z,
):
    set_masks(8, inside, face_y, face_z)
    clear_ends(state)
    dt = step_size(0, timestep, tops)

    def gather(block, carry):
        ok = inside[...] > 0.0
        lane = iota((ROWS, LANES), 1)
        group = lane >> 3
        for j in range(2):
            around = []
            for odd in range(2):
                p = 4 * block + 2 * j + odd
                for which in range(2):
                    at = MAIN_TILES + 8 * which + 2 * block + j
                    tile = halo_tile(high[at], low[at], odd == 1)
                    around.append(jnp.concatenate([sides[which, p], tile], axis=0))
            for f in range(FIELDS + 1):
                tile = halo_tile(high[4 * f + block], low[4 * f + block], j == 1)
                for odd in range(2):
                    p = 4 * block + 2 * j + odd
                    below, above = around[2 * odd], around[2 * odd + 1]
                    value = jnp.concatenate([own[f, p], roll(tile, HALF * odd, 1)], axis=0)
                    side = roll(jnp.where(group == f, above, below), HALF - 8 * f, 1)
                    value = jnp.where(ok, jnp.where(lane < HALF, value, side), 0.0)
                    state[f, p + PAD] = value
                    if f == FIELDS:
                        kinds[p] = value
        return carry

    lax.fori_loop(0, 4, gather, 0)
    strain_pass(dt, state, stress, rest, inside)
    force_pass(dt, state, stress, lead, inside)

    def put(f, p, value):
        out[f, p] = value

    sweep_lead(
        dt, lead, moved, mids, (along_x, along_y, along_z), scales, inside, face_y, face_z, put
    )

    def peaks(p, peak):
        speed = jnp.maximum(jnp.abs(out[1, p]), jnp.abs(out[2, p]))
        speed = jnp.maximum(speed, jnp.abs(out[3, p]))
        kind = kinds[p, :OWN]
        speed = speed + pick(kind == 0.0, kind == 1.0, sound_table)
        lane = iota((OWN, LANES), 1)
        return jnp.maximum(peak, jnp.where(lane < HALF, speed, 0.0))

    peak = lax.fori_loop(0, PLANES, peaks, jnp.zeros((OWN, LANES), jnp.float32))
    top[...] = jnp.full(top.shape, jnp.max(peak), jnp.float32)


def rest_kernel(lead, rest, along_x, along_y, along_z, scales, out, up, down, moved, mids):
    def put(f, p, value):
        out[f, p] = value

    sweep_rest(rest, moved, mids, (along_x, along_y, along_z), scales, put)

    def messages(i, carry):
        for f in range(FIELDS):
            src, at = (lead, LEAD_AT.index(f)) if f in LEAD_AT else (out, REST_AT.index(f))
            even, odd = src[at, 2 * i], src[at, 2 * i + 1]
            up[f, i] = stack_rows(even, odd, True)
            down[f, i] = stack_rows(even, odd, False)
        return carry

    lax.fori_loop(0, PLANES // 2, messages, 0)


def second_kernel(
    timestep, tops, own_lead, own_rest, kinds, low, high, mine, to1, to2, to3,
    state, stress, lead, moved, mids, inside, face_y, face_z,
    rest, rest_moved, rest_mids, along_x, along_y, along_z, scales, out,
):
    set_masks(4, inside, face_y, face_z)
    clear_ends(state)
    dt = step_size(1, timestep, tops)

    def gather(i, carry):
        ok = inside[...] > 0.0
        for f in range(FIELDS):
            src, at = (own_lead, LEAD_AT.index(f)) if f in LEAD_AT else (own_rest, REST_AT.index(f))
            for odd in range(2):
                p = 2 * i + odd
                tile = halo_tile(high[f, i], low[f, i], odd == 1)
                value = jnp.concatenate([src[at, p], tile], axis=0)
                state[f, p + PAD] = jnp.where(ok, value, 0.0)
        for odd in range(2):
            state[FIELDS, 2 * i + odd + PAD] = kinds[2 * i + odd]
        return carry

    lax.fori_loop(0, PLANES // 2, gather, 0)
    strain_pass(dt, state, stress, rest, inside)
    force_pass(dt, state, stress, lead, inside)
    courants = (along_x, along_y, along_z)

    def put_lead(f, p, value):
        out[f, p] = value

    def put_rest(f, p, value):
        out[LEAD + f, p] = value

    sweep_lead(dt, lead, moved, mids, courants, scales, inside, face_y, face_z, put_lead)
    sweep_rest(rest, rest_moved, rest_mids, courants, scales, put_rest)

    left = iota((OWN, LANES), 1) < HALF
    for k, dest in enumerate((mine, to1, to2, to3)):
        block = position()[0] ^ k
        for f in range(FIELDS):
            for j in range(2):
                even, odd = out[ORDER[f], 4 * block + 2 * j], out[ORDER[f], 4 * block + 2 * j + 1]
                dest[f, j] = jnp.where(left, even, roll(odd, HALF, 1))


def unpack_kernel(mine, from1, from2, from3, dens, ener, vel, plas, dama, devi, held):
    me = position()[0]
    refs = [dens, ener] + [vel.at[i] for i in range(3)] + [plas, dama]
    refs = refs + [devi.at[i] for i in range(6)]
    for k, src in enumerate((mine, from1, from2, from3)):
        held[me ^ k] = src[...]
    left = iota((OWN, LANES), 1) < HALF
    for f in range(FIELDS):
        for j in range(2):
            for t in range(2):
                first, second = held[2 * t, f, j], held[2 * t + 1, f, j]
                cols = slice(t * LANES, (t + 1) * LANES)
                refs[f][2 * j, :, cols] = jnp.where(left, first, roll(second, HALF, 1))
                refs[f][2 * j + 1, :, cols] = jnp.where(left, roll(first, HALF, 1), second)


IN_VMEM = pl.BlockSpec(memory_space=pltpu.VMEM)
IN_SMEM = pl.BlockSpec(memory_space=pltpu.SMEM)


def call(kernel, scalars, outs, scratch, *args):
    return pl.pallas_call(
        kernel,
        out_shape=[jax.ShapeDtypeStruct(shape, jnp.float32) for shape in outs],
        in_specs=[IN_SMEM] * scalars + [IN_VMEM] * (len(args) - scalars),
        out_specs=[IN_VMEM] * len(outs),
        scratch_shapes=[pltpu.VMEM(shape, jnp.float32) for shape in scratch],
        compiler_params=pltpu.CompilerParams(vmem_limit_bytes=48 * 1024 * 1024),
    )(*args)


def ring_pair(to_next, to_last, axes, order):
    after = order[1:] + order[:1]
    low = lax.ppermute(to_next, axes, list(zip(order, after)))
    high = lax.ppermute(to_last, axes, list(zip(after, order)))
    return low, high


def swap_blocks(parts):
    count = lax.axis_size("gx")
    return [
        lax.ppermute(part, "gx", [(i, i ^ (k + 1)) for i in range(count)])
        for k, part in enumerate(parts)
    ]


def shards(density, energy, velocity, plastic_strain, damage, deviator, materials, timestep):
    size_y, size_z = lax.axis_size("gy"), lax.axis_size("gz")
    all_fields = FIELDS + 1
    part = (PART_ROWS + 8, LANES)
    inputs = (density, energy, velocity, plastic_strain, damage, deviator, materials)
    edge = (4, OWN, LANES)
    own, *parts, edges, z_up, z_down = pl.pallas_call(
        pack_kernel,
        out_shape=[
            jax.ShapeDtypeStruct(shape, jnp.float32) for shape in [part] * 4 + [(4, 2) + edge, edge, edge]
        ],
        in_specs=[pl.BlockSpec(memory_space=pltpu.HBM)] * len(inputs),
        out_specs=[IN_VMEM] * 7,
        scratch_shapes=[pltpu.VMEM(array.shape, array.dtype) for array in inputs]
        + [pltpu.SemaphoreType.DMA((len(inputs),))],
        compiler_params=pltpu.CompilerParams(vmem_limit_bytes=PACK_LIMIT),
    )(*inputs)
    z_low, z_high = ring_pair(z_up, z_down, "gz", list(range(size_z)))
    parts = swap_blocks(parts)
    own_z, *z_parts = call(edge_kernel, 0, [(2,) + edge] * 4, [], edges, z_low, z_high)
    z_parts = swap_blocks(z_parts)
    message = (MAIN_TILES + PLANES, 8, LANES)
    state, sides, up, down, top = call(
        spread_kernel,
        0,
        [(all_fields, PLANES, OWN, LANES), (2, PLANES, OWN, LANES), message, message]
        + [(size_y * size_z, LANES)],
        [],
        own,
        *parts,
        own_z,
        *z_parts,
    )
    low, high = ring_pair(up, down, "gy", list(range(size_y)))
    tops = lax.all_to_all(top, ("gy", "gz"), 0, 0)
    full = (ROWS, LANES)
    scratch = [
        (all_fields, PLANES + 2 * PAD) + full,
        (6, PLANES + 2) + full,
        (LEAD, PLANES) + full,
        (LEAD, PLANES) + full,
        (2, LEAD, LANES, LANES),
        full,
        full,
        (2, DEPTH, LANES),
    ]
    left_over = [
        (REST, PLANES) + full,
        (PLANES - 1,) + full,
        (PLANES,) + full,
        (2, DEPTH, LANES),
        (2, DEPTH, LANES),
    ]
    rest_scratch = [(REST, PLANES) + full, (2, LANES, LANES)]
    lead, *rest, kinds, top = call(
        lead_kernel,
        1,
        [(LEAD, PLANES, OWN, LANES)] + left_over + [(PLANES,) + full, (8, LANES)],
        scratch,
        timestep,
        tops,
        state,
        sides,
        low,
        high,
    )
    others = swap_blocks([top] * 3)
    rest, up, down = call(
        rest_kernel,
        0,
        [(REST, PLANES, OWN, LANES)] + [(FIELDS, PLANES // 2, 8, LANES)] * 2,
        rest_scratch,
        lead,
        *rest,
    )
    low, high = ring_pair(up, down, "gy", list(range(size_y)))
    for other in others:
        top = jnp.maximum(top, other)
    tops = lax.all_to_all(jnp.broadcast_to(top[:1], (size_y * size_z, LANES)), ("gy", "gz"), 0, 0)
    mine, *parts = call(
        second_kernel,
        1,
        [(FIELDS, 2, OWN, LANES)] * 4,
        scratch + left_over[:1] + rest_scratch + left_over[1:] + [(FIELDS, PLANES, OWN, LANES)],
        timestep,
        tops,
        lead,
        rest,
        kinds,
        low,
        high,
    )
    parts = swap_blocks(parts)
    cells = density.shape
    return tuple(
        call(
            unpack_kernel,
            0,
            [cells, cells, (3,) + cells, cells, cells, (6,) + cells],
            [(4, FIELDS, 2, OWN, LANES)],
            mine,
            *parts,
        )
    )


def solution(mesh):
    cells = P("gx", "gy", "gz")
    vectors = P(None, "gx", "gy", "gz")
    return jax.shard_map(
        shards,
        mesh=mesh,
        in_specs=(cells, cells, vectors, cells, cells, vectors, cells, P()),
        out_specs=(cells, cells, vectors, cells, cells, vectors),
        check_vma=False,
    )
```

```python
import jax
import jax.numpy as jnp
from jax import lax
from jax.experimental import pallas as pl
from jax.experimental.pallas import tpu as pltpu
from jax.sharding import PartitionSpec as P


FIELDS = 13
PLANES = 16
ROWS = 24
OWN = 16
LANES = 128
HALF = 64
DEPTH = 80
GROUP = 8
PAD = 2

shear_table = (1.0, 0.5, 0.8)
sound_table = (1.5, 1.2, 1.0)
gruneisen_table = (2.0, 2.1, 1.9)
rest_table = (4.0, 3.0, 5.0)
yield_table = (0.3, 0.2, 0.25)
harden_table = (0.5, 0.3, 0.4)
exponent_table = (0.3, 0.4, 0.35)
rate_table = (0.02, 0.015, 0.01)
cfl_number = 0.2

PACK_LIMIT = 62 * 1024 * 1024
CALL_LIMIT = 48 * 1024 * 1024
ACROSS = ((0, 3, 5), (3, 1, 4), (5, 4, 2))


def roll(value, shift, axis):
    shift = shift % value.shape[axis]
    return value if shift == 0 else pltpu.roll(value, shift, axis)


def position():
    size_x = lax.axis_size("gx")
    place_x = lax.axis_index("gx")
    chunk = lax.axis_index("gz") * size_x + place_x
    return place_x, lax.axis_index("gy"), chunk, lax.axis_size("gy") - 1, size_x * lax.axis_size("gz") - 1


def iota(shape, axis):
    return lax.broadcasted_iota(jnp.int32, shape, axis)


def inverse(value):
    guess = pl.reciprocal(value, approx=True)
    return guess * (2.0 - value * guess)


def pick(first, second, table):
    return jnp.where(first, table[0], jnp.where(second, table[1], table[2]))


def stack_rows(even, odd, upper):
    low_rows = iota((8, LANES), 0) < 4
    if upper:
        return jnp.where(low_rows, roll(even[8:], 4, 0), odd[8:])
    return jnp.where(low_rows, even[:8], roll(odd[:8], 4, 0))


def halo_tile(high, low, odd):
    low_rows = iota((8, LANES), 0) < 4
    if odd:
        return jnp.where(low_rows, roll(high, 4, 0), low)
    return jnp.where(low_rows, high, roll(low, 4, 0))


PART_ROWS = (FIELDS + 1) * 2 * OWN


def part_rows(f, j):
    return slice((2 * f + j) * OWN, (2 * f + j + 1) * OWN)


def pack_kernel(*args):
    sources, (own, to1, to2, to3, edges, z_up, z_down) = args[:7], args[7:14]
    buffers, arrived = args[14:21], args[21]
    copies = [
        pltpu.make_async_copy(source, buffer, arrived.at[i])
        for i, (source, buffer) in enumerate(zip(sources, buffers))
    ]
    for copy in copies:
        copy.start()
    for copy in copies:
        copy.wait()
    dens, ener, vel, plas, dama, devi, mat = buffers
    me = position()[0]
    refs = [dens, ener] + [vel.at[i] for i in range(3)] + [plas, dama]
    refs = refs + [devi.at[i] for i in range(6)] + [mat]
    peak = None
    for x in range(4):
        for t in range(2):
            cols = slice(t * LANES, (t + 1) * LANES)
            speed = jnp.maximum(jnp.abs(vel[0, x, :, cols]), jnp.abs(vel[1, x, :, cols]))
            speed = jnp.maximum(speed, jnp.abs(vel[2, x, :, cols]))
            kind = mat[x, :, cols]
            speed = speed + pick(kind == 0, kind == 1, sound_table)
            peak = speed if peak is None else jnp.maximum(peak, speed)
    peak = jnp.full((8, LANES), jnp.max(peak), jnp.float32)
    left = iota((OWN, LANES), 1) < HALF
    for k, out in enumerate((own, to1, to2, to3)):
        out[PART_ROWS:] = peak
        target = me ^ k
        cols = pl.ds(pl.multiple_of((target >> 1) * LANES, LANES), LANES)
        odd = target & 1
        side = left == (odd == 0)
        for f in range(FIELDS + 1):
            for j in range(2):
                even_plane = refs[f][2 * j, :, cols].astype(jnp.float32)
                odd_plane = refs[f][2 * j + 1, :, cols].astype(jnp.float32)
                stays = jnp.where(odd == 1, odd_plane, even_plane)
                turns = jnp.where(odd == 1, even_plane, odd_plane)
                out[part_rows(f, j)] = jnp.where(side, stays, roll(turns, HALF, 1))

    group = iota((OWN, LANES), 1) >> 3

    def plane(x, carry):
        zero = jnp.zeros((OWN, LANES), jnp.float32)
        below, above = [zero] * 5, [zero] * 5
        for f in range(FIELDS + 1):
            in_below, in_above = group == (f + 7) % 16, group == f
            for t in range(2):
                tile = refs[f][x, :, t * LANES : (t + 1) * LANES].astype(jnp.float32)
                near, far = roll(tile, 8 * f, 1), roll(tile, 8 * f - HALF, 1)
                below[2 * t + 1] = jnp.where(in_below, near, below[2 * t + 1])
                below[2 * t + 2] = jnp.where(in_below, far, below[2 * t + 2])
                above[2 * t] = jnp.where(in_above, near, above[2 * t])
                above[2 * t + 1] = jnp.where(in_above, far, above[2 * t + 1])
        for g in range(4):
            edges[g, 0, x] = below[g]
            edges[g, 1, x] = above[g + 1]
        z_up[x] = below[4]
        z_down[x] = above[0]
        return carry

    lax.fori_loop(0, 4, plane, 0)


def edge_kernel(edges, from_below, from_above, own, to1, to2, to3):
    me = position()[0]
    for k, out in enumerate((own, to1, to2, to3)):
        target = me ^ k
        out[0] = jnp.where(target == 0, from_below[...], edges[target, 0])
        out[1] = jnp.where(target == 3, from_above[...], edges[target, 1])


MAIN_TILES = (FIELDS + 1) * 4


def spread_kernel(own, from1, from2, from3, own_z, z1, z2, z3, state, sides, up, down, top):
    me = position()[0]
    peak = jnp.maximum(
        jnp.maximum(own[PART_ROWS:], from1[PART_ROWS:]), jnp.maximum(from2[PART_ROWS:], from3[PART_ROWS:])
    )
    top[...] = jnp.broadcast_to(peak[:1], top.shape)
    for k, (src, side) in enumerate(((own, own_z), (from1, z1), (from2, z2), (from3, z3))):
        block = me ^ k
        for f in range(FIELDS + 1):
            first, second = src[part_rows(f, 0)], src[part_rows(f, 1)]
            state[f, 4 * block] = first
            state[f, 4 * block + 1] = roll(first, HALF, 1)
            state[f, 4 * block + 2] = second
            state[f, 4 * block + 3] = roll(second, HALF, 1)
            up[4 * f + block] = stack_rows(first, second, True)
            down[4 * f + block] = stack_rows(first, second, False)
        for which in range(2):
            for j in range(2):
                even, odd = side[which, 2 * j], side[which, 2 * j + 1]
                sides[which, 4 * block + 2 * j] = even
                sides[which, 4 * block + 2 * j + 1] = odd
                at = MAIN_TILES + 8 * which + 2 * block + j
                up[at] = stack_rows(even, odd, True)
                down[at] = stack_rows(even, odd, False)


def set_masks(width, inside, face_y, face_z):
    _, place_y, chunk, last_y, last_chunk = position()
    shape = (ROWS, LANES)
    row, lane = iota(shape, 0), iota(shape, 1)
    row_ok = (row < OWN) | ((row < OWN + 4) & (place_y < last_y)) | ((row >= OWN + 4) & (place_y > 0))
    lane_ok = (
        (lane < HALF)
        | ((lane < HALF + width) & (chunk < last_chunk))
        | ((lane >= LANES - width) & (chunk > 0))
    )
    ok = jnp.where(row_ok & lane_ok, 1.0, 0.0)
    inside[...] = ok
    face_y[...] = ok * roll(ok, -1, 0)
    row = iota((DEPTH, LANES), 0)
    row_ok = (
        (row < HALF)
        | ((row < HALF + width) & (chunk < last_chunk))
        | ((row >= DEPTH - width) & (chunk > 0))
    )
    ok = jnp.where(row_ok, 1.0, 0.0)
    face_z[0] = ok
    face_z[1] = ok * roll(ok, -1, 0)


def step_size(step_no, timestep, tops):
    top_speed = jnp.max(tops[...], axis=0, keepdims=True)
    asked = timestep[step_no]
    return asked / (1.0 + asked * top_speed / cfl_number)


def central(upper, lower):
    return 0.5 * (upper - lower)


def limited(back, fore):
    product = back * fore
    return jnp.where(product > 0.0, product * inverse(back + fore), 0.0)


def carried(positive, here, there, slope_here, slope_there, courant, weight):
    return courant * (
        jnp.where(positive, here, there) + weight * jnp.where(positive, slope_here, slope_there)
    )


def weigh(courant):
    return jnp.where(courant > 0.0, 1.0, -1.0) - courant


def rolled_change(q, positive, courant, weight):
    q_next = roll(q, -1, 0)
    fore = q_next - q
    slope = limited(roll(fore, 1, 0), fore)
    flux = carried(positive, q, q_next, slope, roll(slope, -1, 0), courant, weight)
    return q - (flux - roll(flux, 1, 0))


def rolled_courant(dt, density, momentum, closed):
    velocity = momentum * inverse(density)
    return dt * 0.5 * (velocity + roll(velocity, -1, 0)) * closed


def strain_at(dt, p, state, stress, rest, inside):
    at = p + PAD
    ok = inside[...] > 0.0
    vel = [state[2 + i, at] for i in range(3)]
    grad = [
        [
            central(state[2 + i, at + 1], state[2 + i, at - 1]),
            central(roll(vel[i], -1, 0), roll(vel[i], 1, 0)),
            central(roll(vel[i], -1, 1), roll(vel[i], 1, 1)),
        ]
        for i in range(3)
    ]
    third_div = (grad[0][0] + grad[1][1] + grad[2][2]) * (1.0 / 3.0)
    strain = [
        grad[0][0] - third_div,
        grad[1][1] - third_div,
        grad[2][2] - third_div,
        0.5 * (grad[0][1] + grad[1][0]),
        0.5 * (grad[1][2] + grad[2][1]),
        0.5 * (grad[0][2] + grad[2][0]),
    ]
    kind = state[FIELDS, at]
    first, second = kind == 0.0, kind == 1.0
    density, energy = state[0, at], state[1, at]
    plastic, damage = state[5, at], state[6, at]
    pressure = (
        pick(first, second, tuple(c * c for c in sound_table))
        * (density - pick(first, second, rest_table))
        + pick(first, second, gruneisen_table) * density * energy
    )
    shear_dt = pick(first, second, tuple(2.0 * g for g in shear_table)) * dt
    trial = [state[7 + k, at] + shear_dt * strain[k] for k in range(6)]
    trial_sq = (
        trial[0] * trial[0]
        + trial[1] * trial[1]
        + trial[2] * trial[2]
        + 2.0 * (trial[3] * trial[3] + trial[4] * trial[4] + trial[5] * trial[5])
    )
    strain_sq = (
        strain[0] * strain[0]
        + strain[1] * strain[1]
        + strain[2] * strain[2]
        + 2.0 * (strain[3] * strain[3] + strain[4] * strain[4] + strain[5] * strain[5])
    )
    equivalent = jnp.sqrt(1.5 * trial_sq)
    strain_rate = jnp.sqrt(strain_sq * (2.0 / 3.0))
    hardened = pick(first, second, yield_table) + pick(first, second, harden_table) * jnp.exp(
        pick(first, second, exponent_table) * jnp.log(plastic)
    )
    flow = (
        hardened
        * (1.0 + pick(first, second, rate_table) * jnp.log(1.0 + strain_rate))
        * (1.0 - damage)
    )
    bound = jnp.maximum(equivalent, flow)
    per_bound = inverse(bound)
    factor = flow * per_bound
    increment = (bound - flow) * pick(first, second, tuple(1.0 / (3.0 * g) for g in shear_table))
    triaxial = jnp.clip(-pressure * per_bound, -1.5, 1.5)
    failure = 0.05 + 0.8 * jnp.exp(-1.5 * triaxial)
    rest[1, p] = jnp.where(ok, density * (plastic + increment), 0.0)
    worn = jnp.minimum(damage + increment * inverse(failure), 0.9)
    rest[2, p] = jnp.where(ok, density * worn, 0.0)
    dev = [jnp.where(ok, trial[k] * factor, 0.0) for k in range(6)]
    held = jnp.where(ok, pressure, 0.0)
    full = [dev[0] - held, dev[1] - held, dev[2] - held, dev[3], dev[4], dev[5]]
    for k in range(6):
        rest[3 + k, p] = density * dev[k]
        stress[k, p + 1] = full[k]
    work = (
        full[0] * grad[0][0]
        + full[1] * grad[1][1]
        + full[2] * grad[2][2]
        + 2.0 * (full[3] * strain[3] + full[4] * strain[4] + full[5] * strain[5])
    )
    rest[0, p] = jnp.where(ok, density * energy + dt * work, 0.0)
    return full


def force_at(dt, p, state, stress, lead, inside, ahead):
    density = state[0, p + PAD]
    here = [stress[k, p + 1] for k in range(6)]
    lead[0, p] = density
    for i in range(3):
        along_x, along_y, along_z = ACROSS[0][i], ACROSS[1][i], ACROSS[2][i]
        force = (
            central(ahead[along_x], stress[along_x, p])
            + central(roll(here[along_y], -1, 0), roll(here[along_y], 1, 0))
            + central(roll(here[along_z], -1, 1), roll(here[along_z], 1, 1))
        )
        pushed = jnp.where(inside[...] > 0.0, dt * force, 0.0)
        lead[1 + i, p] = density * state[2 + i, p + PAD] + pushed


def stress_and_force(dt, gather, state, stress, rest, lead, inside):
    zero = jnp.zeros((ROWS, LANES), jnp.float32)
    for k in range(6):
        stress[k, 0] = zero
    gather(0, 0, PAD)
    gather(0, 1, PAD + 1)

    def block(b, carry):
        for i in range(4):
            p = 4 * b + i
            full = strain_at(dt, p, state, stress, rest, inside)
            if i > 0:
                force_at(dt, p - 1, state, stress, lead, inside, full)
            else:
                force_at(dt, jnp.maximum(p - 1, 0), state, stress, lead, inside, full)
            soon = p + 2
            to = jnp.where(soon < PLANES, soon + PAD, PLANES + 2 * PAD - 1)
            gather(jnp.minimum(b + (i + 2) // 4, 3), (i + 2) % 4, to)
        return carry

    lax.fori_loop(0, PLANES // 4, block, 0)
    force_at(dt, PLANES - 1, state, stress, lead, inside, [zero] * 6)


def first_sweep(fields, f, moved, courants):
    here = fields[f, 0]
    ahead = fields[f, 1]
    fore = ahead - here
    slope = limited(here, fore)
    last_flux = None
    for p in range(PLANES - 1):
        further = fields[f, p + 2] if p + 2 < PLANES else 0.0
        next_fore = further - ahead
        next_slope = limited(fore, next_fore)
        courant = courants[p]
        flux = carried(courant > 0.0, here, ahead, slope, next_slope, courant, weigh(courant))
        moved[f, p] = here - (flux if last_flux is None else flux - last_flux)
        last_flux, here, ahead, fore, slope = flux, ahead, further, next_fore, next_slope
    moved[f, PLANES - 1] = here + last_flux


def first_courants(dt, lead, courants, inside):
    ok = inside[...] > 0.0
    here = None
    for p in range(PLANES):
        ahead = lead[1, p] * inverse(jnp.where(ok, lead[0, p], 1.0))
        if p > 0:
            courants[p - 1] = dt * 0.5 * (here + ahead)
        here = ahead


def second_sweep(moved, f, group, courant_of, mid):
    for i in range(GROUP):
        p = GROUP * group + i
        courant = courant_of(p)
        value = rolled_change(moved[f, p], courant > 0.0, courant, weigh(courant))
        mid[OWN * i : OWN * (i + 1)] = value[:OWN]


def turned(mid):
    value = mid[...].T
    return jnp.concatenate([value[: HALF + 8], value[LANES - 8 :]], axis=0)


def turn_back(value, put, f, group):
    gap = jnp.zeros((LANES - DEPTH, LANES), jnp.float32)
    value = jnp.concatenate([value[: HALF + 8], gap, value[HALF + 8 :]], axis=0).T
    for i in range(GROUP):
        put(f, GROUP * group + i, value[OWN * i : OWN * (i + 1)])


LEAD = 4
REST = 9
LEAD_AT = (0, 2, 3, 4)
REST_AT = (1, 5, 6, 7, 8, 9, 10, 11, 12)
ORDER = tuple((LEAD_AT + REST_AT).index(f) for f in range(FIELDS))


def sweep_lead(dt, lead, moved, mids, courants, scales, inside, face_y, face_z, put):
    along_x, along_y, along_z = courants
    first_courants(dt, lead, along_x, inside)
    for f in range(LEAD):
        first_sweep(lead, f, moved, along_x)

    def second_courant(p):
        density = jnp.where(inside[...] > 0.0, moved[0, p], 1.0)
        courant = rolled_courant(dt, density, moved[2, p], face_y[...])
        along_y[p] = courant
        return courant

    def second(group):
        second_sweep(moved, 0, group, second_courant, mids.at[group, 0])
        for f in range(1, LEAD):
            second_sweep(moved, f, group, lambda p: along_y[p], mids.at[group, f])

    def third(group):
        ok = face_z[0] > 0.0
        density = turned(mids.at[group, 0])
        momentum = turned(mids.at[group, 3])
        courant = rolled_courant(dt, jnp.where(ok, density, 1.0), momentum, face_z[1])
        along_z[group] = courant
        positive, weight = courant > 0.0, weigh(courant)
        value = rolled_change(density, positive, courant, weight)
        scale = jnp.where(ok, inverse(jnp.where(ok, value, 1.0)), 0.0)
        scales[group] = scale
        turn_back(jnp.where(ok, value, 0.0), put, 0, group)
        for f in range(1, LEAD):
            value = turned(mids.at[group, f]) if f < 3 else momentum
            turn_back(rolled_change(value, positive, courant, weight) * scale, put, f, group)

    second(0)
    second(1)
    third(0)
    third(1)


def sweep_rest(rest, moved, mids, courants, scales, put):
    along_x, along_y, along_z = courants
    last = REST - 1

    def second(f, group):
        second_sweep(moved, f, group, lambda p: along_y[p], mids.at[group])

    def field(f, carry):
        for group in range(2):
            courant = along_z[group]
            value = rolled_change(turned(mids.at[group]), courant > 0.0, courant, weigh(courant))
            turn_back(value * scales[group], put, f, group)
            second(jnp.minimum(f + 1, last), group)
        return carry

    def first(f, carry):
        first_sweep(rest, f, moved, along_x)
        return carry

    lax.fori_loop(0, REST, first, 0)
    for group in range(2):
        second(0, group)
    lax.fori_loop(0, REST, field, 0)


def clear_ends(state):
    zero = jnp.zeros((ROWS, LANES), jnp.float32)
    for f in range(FIELDS + 1):
        for p in (0, 1, PLANES + PAD, PLANES + PAD + 1):
            state[f, p] = zero


def lead_kernel(
    timestep, tops, own, sides, low, high, out, rest, along_x, along_y, along_z, scales, kinds, top,
    state, stress, lead, moved, mids, inside, face_y, face_z,
):
    set_masks(8, inside, face_y, face_z)
    clear_ends(state)
    dt = step_size(0, timestep, tops)

    def gather(block, i, to):
        j, odd = i // 2, i % 2
        p = 4 * block + i
        ok = inside[...] > 0.0
        lane = iota((ROWS, LANES), 1)
        group = lane >> 3
        around = []
        for which in range(2):
            at = MAIN_TILES + 8 * which + 2 * block + j
            tile = halo_tile(high[at], low[at], odd == 1)
            around.append(jnp.concatenate([sides[which, p], tile], axis=0))
        for f in range(FIELDS + 1):
            tile = roll(halo_tile(high[4 * f + block], low[4 * f + block], j == 1), HALF * odd, 1)
            value = jnp.concatenate([own[f, p], tile], axis=0)
            side = roll(jnp.where(group == f, around[1], around[0]), HALF - 8 * f, 1)
            value = jnp.where(ok, jnp.where(lane < HALF, value, side), 0.0)
            state[f, to] = value
            if f == FIELDS:
                kinds[p] = value

    stress_and_force(dt, gather, state, stress, rest, lead, inside)

    def put(f, p, value):
        out[f, p] = value

    sweep_lead(
        dt, lead, moved, mids, (along_x, along_y, along_z), scales, inside, face_y, face_z, put
    )

    def peaks(p, peak):
        speed = jnp.maximum(jnp.abs(out[1, p]), jnp.abs(out[2, p]))
        speed = jnp.maximum(speed, jnp.abs(out[3, p]))
        kind = kinds[p, :OWN]
        speed = speed + pick(kind == 0.0, kind == 1.0, sound_table)
        lane = iota((OWN, LANES), 1)
        return jnp.maximum(peak, jnp.where(lane < HALF, speed, 0.0))

    peak = lax.fori_loop(0, PLANES, peaks, jnp.zeros((OWN, LANES), jnp.float32))
    top[...] = jnp.full(top.shape, jnp.max(peak), jnp.float32)


def rest_kernel(lead, rest, along_x, along_y, along_z, scales, out, up, down, moved, mids):
    def put(f, p, value):
        out[f, p] = value

    sweep_rest(rest, moved, mids, (along_x, along_y, along_z), scales, put)

    def messages(i, carry):
        for f in range(FIELDS):
            src, at = (lead, LEAD_AT.index(f)) if f in LEAD_AT else (out, REST_AT.index(f))
            even, odd = src[at, 2 * i], src[at, 2 * i + 1]
            up[f, i] = stack_rows(even, odd, True)
            down[f, i] = stack_rows(even, odd, False)
        return carry

    lax.fori_loop(0, PLANES // 2, messages, 0)


def second_kernel(
    timestep, tops, own_lead, own_rest, kinds, low, high, mine, to1, to2, to3,
    state, stress, lead, moved, mids, inside, face_y, face_z,
    rest, rest_moved, rest_mids, along_x, along_y, along_z, scales, out,
):
    set_masks(4, inside, face_y, face_z)
    clear_ends(state)
    dt = step_size(1, timestep, tops)

    def gather(block, i, to):
        p = 4 * block + i
        pair, odd = 2 * block + i // 2, i % 2
        ok = inside[...] > 0.0
        for f in range(FIELDS):
            src, at = (own_lead, LEAD_AT.index(f)) if f in LEAD_AT else (own_rest, REST_AT.index(f))
            tile = halo_tile(high[f, pair], low[f, pair], odd == 1)
            state[f, to] = jnp.where(ok, jnp.concatenate([src[at, p], tile], axis=0), 0.0)
        state[FIELDS, to] = kinds[p]

    stress_and_force(dt, gather, state, stress, rest, lead, inside)
    courants = (along_x, along_y, along_z)

    def put_lead(f, p, value):
        out[f, p] = value

    def put_rest(f, p, value):
        out[LEAD + f, p] = value

    sweep_lead(dt, lead, moved, mids, courants, scales, inside, face_y, face_z, put_lead)
    sweep_rest(rest, rest_moved, rest_mids, courants, scales, put_rest)
    me = position()[0]
    for k, part in enumerate((mine, to1, to2, to3)):
        pack_block(out, me ^ k, part)


def pack_block(out, block, part):
    left = iota((OWN, LANES), 1) < HALF
    first = 4 * block
    for f in range(FIELDS):
        for j in range(2):
            even, odd = out[ORDER[f], first + 2 * j], out[ORDER[f], first + 2 * j + 1]
            part[f, j] = jnp.where(left, even, roll(odd, HALF, 1))


def unpack_kernel(mine, from1, from2, from3, dens, ener, vel, plas, dama, devi, held):
    me = position()[0]
    refs = [dens, ener] + [vel.at[i] for i in range(3)] + [plas, dama]
    refs = refs + [devi.at[i] for i in range(6)]
    for k, src in enumerate((mine, from1, from2, from3)):
        held[me ^ k] = src[...]
    left = iota((OWN, LANES), 1) < HALF
    for f in range(FIELDS):
        for j in range(2):
            for t in range(2):
                first, second = held[2 * t, f, j], held[2 * t + 1, f, j]
                cols = slice(t * LANES, (t + 1) * LANES)
                refs[f][2 * j, :, cols] = jnp.where(left, first, roll(second, HALF, 1))
                refs[f][2 * j + 1, :, cols] = jnp.where(left, roll(first, HALF, 1), second)


IN_VMEM = pl.BlockSpec(memory_space=pltpu.VMEM)
IN_SMEM = pl.BlockSpec(memory_space=pltpu.SMEM)


def call(kernel, scalars, outs, scratch, *args, micros=1):
    return pl.pallas_call(
        kernel,
        out_shape=[jax.ShapeDtypeStruct(shape, jnp.float32) for shape in outs],
        in_specs=[IN_SMEM] * scalars + [IN_VMEM] * (len(args) - scalars),
        out_specs=[IN_VMEM] * len(outs),
        scratch_shapes=[pltpu.VMEM(shape, jnp.float32) for shape in scratch],
        compiler_params=pltpu.CompilerParams(vmem_limit_bytes=CALL_LIMIT),
        cost_estimate=pl.CostEstimate(flops=0, bytes_accessed=micros * 3_600_000, transcendentals=0),
    )(*args)


def ring_pair(to_next, to_last, axes, order):
    after = order[1:] + order[:1]
    low = lax.ppermute(to_next, axes, list(zip(order, after)))
    high = lax.ppermute(to_last, axes, list(zip(after, order)))
    return low, high


def swap_block(part, k):
    return lax.ppermute(part, "gx", [(i, i ^ k) for i in range(lax.axis_size("gx"))])


def swap_blocks(parts):
    return [swap_block(part, k + 1) for k, part in enumerate(parts)]


def shards(density, energy, velocity, plastic_strain, damage, deviator, materials, timestep):
    size_y, size_z = lax.axis_size("gy"), lax.axis_size("gz")
    all_fields = FIELDS + 1
    part = (PART_ROWS + 8, LANES)
    inputs = (density, energy, velocity, plastic_strain, damage, deviator, materials)
    edge = (4, OWN, LANES)
    own, *parts, edges, z_up, z_down = pl.pallas_call(
        pack_kernel,
        out_shape=[
            jax.ShapeDtypeStruct(shape, jnp.float32) for shape in [part] * 4 + [(4, 2) + edge, edge, edge]
        ],
        in_specs=[pl.BlockSpec(memory_space=pltpu.HBM)] * len(inputs),
        out_specs=[IN_VMEM] * 7,
        scratch_shapes=[pltpu.VMEM(array.shape, array.dtype) for array in inputs]
        + [pltpu.SemaphoreType.DMA((len(inputs),))],
        compiler_params=pltpu.CompilerParams(vmem_limit_bytes=PACK_LIMIT),
    )(*inputs)
    z_low, z_high = ring_pair(z_up, z_down, "gz", list(range(size_z)))
    parts = swap_blocks(parts)
    own_z, *z_parts = call(edge_kernel, 0, [(2,) + edge] * 4, [], edges, z_low, z_high)
    z_parts = swap_blocks(z_parts)
    message = (MAIN_TILES + PLANES, 8, LANES)
    state, sides, up, down, top = call(
        spread_kernel,
        0,
        [(all_fields, PLANES, OWN, LANES), (2, PLANES, OWN, LANES), message, message]
        + [(size_y * size_z, LANES)],
        [],
        own,
        *parts,
        own_z,
        *z_parts,
    )
    low, high = ring_pair(up, down, "gy", list(range(size_y)))
    tops = lax.all_to_all(top, ("gy", "gz"), 0, 0)
    full = (ROWS, LANES)
    scratch = [
        (all_fields, PLANES + 2 * PAD) + full,
        (6, PLANES + 2) + full,
        (LEAD, PLANES) + full,
        (LEAD, PLANES) + full,
        (2, LEAD, LANES, LANES),
        full,
        full,
        (2, DEPTH, LANES),
    ]
    left_over = [
        (REST, PLANES) + full,
        (PLANES - 1,) + full,
        (PLANES,) + full,
        (2, DEPTH, LANES),
        (2, DEPTH, LANES),
    ]
    rest_scratch = [(REST, PLANES) + full, (2, LANES, LANES)]
    lead, *rest, kinds, top = call(
        lead_kernel,
        1,
        [(LEAD, PLANES, OWN, LANES)] + left_over + [(PLANES,) + full, (8, LANES)],
        scratch,
        timestep,
        tops,
        state,
        sides,
        low,
        high,
    )
    others = swap_blocks([top] * 3)
    rest, up, down = call(
        rest_kernel,
        0,
        [(REST, PLANES, OWN, LANES)] + [(FIELDS, PLANES // 2, 8, LANES)] * 2,
        rest_scratch,
        lead,
        *rest,
        micros=5,
    )
    low, high = ring_pair(up, down, "gy", list(range(size_y)))
    for other in others:
        top = jnp.maximum(top, other)
    tops = lax.all_to_all(jnp.broadcast_to(top[:1], (size_y * size_z, LANES)), ("gy", "gz"), 0, 0)
    mine, *parts = call(
        second_kernel,
        1,
        [(FIELDS, 2, OWN, LANES)] * 4,
        scratch + left_over[:1] + rest_scratch + left_over[1:] + [(FIELDS, PLANES, OWN, LANES)],
        timestep,
        tops,
        lead,
        rest,
        kinds,
        low,
        high,
    )
    parts = swap_blocks(parts)
    cells = density.shape
    return tuple(
        call(
            unpack_kernel,
            0,
            [cells, cells, (3,) + cells, cells, cells, (6,) + cells],
            [(4, FIELDS, 2, OWN, LANES)],
            mine,
            *parts,
        )
    )


def solution(mesh):
    cells = P("gx", "gy", "gz")
    vectors = P(None, "gx", "gy", "gz")
    return jax.shard_map(
        shards,
        mesh=mesh,
        in_specs=(cells, cells, vectors, cells, cells, vectors, cells, P()),
        out_specs=(cells, cells, vectors, cells, cells, vectors),
        check_vma=False,
    )
```

```python
import jax
import jax.numpy as jnp
from jax import lax
from jax.experimental import pallas as pl
from jax.experimental.pallas import tpu as pltpu
from jax.sharding import PartitionSpec as P


FIELDS = 13
PLANES = 16
ROWS = 24
OWN = 16
LANES = 128
HALF = 64
DEPTH = 80
GROUP = 8
PAD = 2

shear_table = (1.0, 0.5, 0.8)
sound_table = (1.5, 1.2, 1.0)
gruneisen_table = (2.0, 2.1, 1.9)
rest_table = (4.0, 3.0, 5.0)
yield_table = (0.3, 0.2, 0.25)
harden_table = (0.5, 0.3, 0.4)
exponent_table = (0.3, 0.4, 0.35)
rate_table = (0.02, 0.015, 0.01)
cfl_number = 0.2

PACK_LIMIT = 62 * 1024 * 1024
CALL_LIMIT = 48 * 1024 * 1024
ACROSS = ((0, 3, 5), (3, 1, 4), (5, 4, 2))


def roll(value, shift, axis):
    shift = shift % value.shape[axis]
    return value if shift == 0 else pltpu.roll(value, shift, axis)


def position():
    size_x = lax.axis_size("gx")
    place_x = lax.axis_index("gx")
    chunk = lax.axis_index("gz") * size_x + place_x
    return place_x, lax.axis_index("gy"), chunk, lax.axis_size("gy") - 1, size_x * lax.axis_size("gz") - 1


def iota(shape, axis):
    return lax.broadcasted_iota(jnp.int32, shape, axis)


def inverse(value):
    return pltpu.reciprocal(value, approx=True)


def pick(first, second, table):
    return jnp.where(first, table[0], jnp.where(second, table[1], table[2]))


def stack_rows(even, odd, upper):
    low_rows = iota((8, LANES), 0) < 4
    if upper:
        return jnp.where(low_rows, roll(even[8:], 4, 0), odd[8:])
    return jnp.where(low_rows, even[:8], roll(odd[:8], 4, 0))


def halo_tile(high, low, odd):
    low_rows = iota((8, LANES), 0) < 4
    if odd:
        return jnp.where(low_rows, roll(high, 4, 0), low)
    return jnp.where(low_rows, high, roll(low, 4, 0))


PART_ROWS = (FIELDS + 1) * 2 * OWN


def part_rows(f, j):
    return slice((2 * f + j) * OWN, (2 * f + j + 1) * OWN)


def pack_kernel(*args):
    sources, (own, to1, to2, to3, edges, z_up, z_down) = args[:7], args[7:14]
    buffers, arrived = args[14:21], args[21]
    copies = [
        pltpu.make_async_copy(source, buffer, arrived.at[i])
        for i, (source, buffer) in enumerate(zip(sources, buffers))
    ]
    for copy in copies:
        copy.start()
    for copy in copies:
        copy.wait()
    dens, ener, vel, plas, dama, devi, mat = buffers
    me = position()[0]
    refs = [dens, ener] + [vel.at[i] for i in range(3)] + [plas, dama]
    refs = refs + [devi.at[i] for i in range(6)] + [mat]
    peak = None
    for x in range(4):
        for t in range(2):
            cols = slice(t * LANES, (t + 1) * LANES)
            speed = jnp.maximum(jnp.abs(vel[0, x, :, cols]), jnp.abs(vel[1, x, :, cols]))
            speed = jnp.maximum(speed, jnp.abs(vel[2, x, :, cols]))
            kind = mat[x, :, cols]
            speed = speed + pick(kind == 0, kind == 1, sound_table)
            peak = speed if peak is None else jnp.maximum(peak, speed)
    peak = jnp.full((8, LANES), jnp.max(peak), jnp.float32)
    left = iota((OWN, LANES), 1) < HALF
    for k, out in enumerate((own, to1, to2, to3)):
        out[PART_ROWS:] = peak
        target = me ^ k
        cols = pl.ds(pl.multiple_of((target >> 1) * LANES, LANES), LANES)
        odd = target & 1
        side = left == (odd == 0)
        for f in range(FIELDS + 1):
            for j in range(2):
                even_plane = refs[f][2 * j, :, cols].astype(jnp.float32)
                odd_plane = refs[f][2 * j + 1, :, cols].astype(jnp.float32)
                stays = jnp.where(odd == 1, odd_plane, even_plane)
                turns = jnp.where(odd == 1, even_plane, odd_plane)
                out[part_rows(f, j)] = jnp.where(side, stays, roll(turns, HALF, 1))

    group = iota((OWN, LANES), 1) >> 3

    def plane(x, carry):
        zero = jnp.zeros((OWN, LANES), jnp.float32)
        below, above = [zero] * 5, [zero] * 5
        for f in range(FIELDS + 1):
            in_below, in_above = group == (f + 7) % 16, group == f
            for t in range(2):
                tile = refs[f][x, :, t * LANES : (t + 1) * LANES].astype(jnp.float32)
                near, far = roll(tile, 8 * f, 1), roll(tile, 8 * f - HALF, 1)
                below[2 * t + 1] = jnp.where(in_below, near, below[2 * t + 1])
                below[2 * t + 2] = jnp.where(in_below, far, below[2 * t + 2])
                above[2 * t] = jnp.where(in_above, near, above[2 * t])
                above[2 * t + 1] = jnp.where(in_above, far, above[2 * t + 1])
        for g in range(4):
            edges[g, 0, x] = below[g]
            edges[g, 1, x] = above[g + 1]
        z_up[x] = below[4]
        z_down[x] = above[0]
        return carry

    lax.fori_loop(0, 4, plane, 0)


def edge_kernel(edges, from_below, from_above, own, to1, to2, to3):
    me = position()[0]
    for k, out in enumerate((own, to1, to2, to3)):
        target = me ^ k
        out[0] = jnp.where(target == 0, from_below[...], edges[target, 0])
        out[1] = jnp.where(target == 3, from_above[...], edges[target, 1])


MAIN_TILES = (FIELDS + 1) * 4


def spread_kernel(own, from1, from2, from3, own_z, z1, z2, z3, state, sides, up, down, top):
    me = position()[0]
    peak = jnp.maximum(
        jnp.maximum(own[PART_ROWS:], from1[PART_ROWS:]), jnp.maximum(from2[PART_ROWS:], from3[PART_ROWS:])
    )
    top[...] = jnp.broadcast_to(peak[:1], top.shape)
    for k, (src, side) in enumerate(((own, own_z), (from1, z1), (from2, z2), (from3, z3))):
        block = me ^ k
        for f in range(FIELDS + 1):
            first, second = src[part_rows(f, 0)], src[part_rows(f, 1)]
            state[f, 4 * block] = first
            state[f, 4 * block + 1] = roll(first, HALF, 1)
            state[f, 4 * block + 2] = second
            state[f, 4 * block + 3] = roll(second, HALF, 1)
            up[4 * f + block] = stack_rows(first, second, True)
            down[4 * f + block] = stack_rows(first, second, False)
        for which in range(2):
            for j in range(2):
                even, odd = side[which, 2 * j], side[which, 2 * j + 1]
                sides[which, 4 * block + 2 * j] = even
                sides[which, 4 * block + 2 * j + 1] = odd
                at = MAIN_TILES + 8 * which + 2 * block + j
                up[at] = stack_rows(even, odd, True)
                down[at] = stack_rows(even, odd, False)


def set_masks(width, inside, face_y, face_z):
    _, place_y, chunk, last_y, last_chunk = position()
    shape = (ROWS, LANES)
    row, lane = iota(shape, 0), iota(shape, 1)
    row_ok = (row < OWN) | ((row < OWN + 4) & (place_y < last_y)) | ((row >= OWN + 4) & (place_y > 0))
    lane_ok = (
        (lane < HALF)
        | ((lane < HALF + width) & (chunk < last_chunk))
        | ((lane >= LANES - width) & (chunk > 0))
    )
    ok = jnp.where(row_ok & lane_ok, 1.0, 0.0)
    inside[...] = ok
    face_y[...] = ok * roll(ok, -1, 0)
    row = iota((DEPTH, LANES), 0)
    row_ok = (
        (row < HALF)
        | ((row < HALF + width) & (chunk < last_chunk))
        | ((row >= DEPTH - width) & (chunk > 0))
    )
    ok = jnp.where(row_ok, 1.0, 0.0)
    face_z[0] = ok
    face_z[1] = ok * roll(ok, -1, 0)


def step_size(step_no, timestep, tops):
    top_speed = jnp.max(tops[...], axis=0, keepdims=True)
    asked = timestep[step_no]
    return asked / (1.0 + asked * top_speed / cfl_number)


def central(upper, lower):
    return 0.5 * (upper - lower)


def limited(back, fore):
    product = back * fore
    return jnp.where(product > 0.0, product * inverse(back + fore), 0.0)


def carried(positive, here, there, slope_here, slope_there, courant, weight):
    return courant * (
        jnp.where(positive, here, there) + weight * jnp.where(positive, slope_here, slope_there)
    )


def weigh(courant):
    return jnp.where(courant > 0.0, 1.0, -1.0) - courant


def rolled_change(q, positive, courant, weight):
    q_next = roll(q, -1, 0)
    fore = q_next - q
    slope = limited(roll(fore, 1, 0), fore)
    flux = carried(positive, q, q_next, slope, roll(slope, -1, 0), courant, weight)
    return q - (flux - roll(flux, 1, 0))


def rolled_courant(dt, density, momentum, closed):
    velocity = momentum * inverse(density)
    return dt * 0.5 * (velocity + roll(velocity, -1, 0)) * closed


def strain_at(dt, p, state, stress, rest, inside):
    at = p + PAD
    ok = inside[...] > 0.0
    vel = [state[2 + i, at] for i in range(3)]
    grad = [
        [
            central(state[2 + i, at + 1], state[2 + i, at - 1]),
            central(roll(vel[i], -1, 0), roll(vel[i], 1, 0)),
            central(roll(vel[i], -1, 1), roll(vel[i], 1, 1)),
        ]
        for i in range(3)
    ]
    third_div = (grad[0][0] + grad[1][1] + grad[2][2]) * (1.0 / 3.0)
    strain = [
        grad[0][0] - third_div,
        grad[1][1] - third_div,
        grad[2][2] - third_div,
        0.5 * (grad[0][1] + grad[1][0]),
        0.5 * (grad[1][2] + grad[2][1]),
        0.5 * (grad[0][2] + grad[2][0]),
    ]
    kind = state[FIELDS, at]
    first, second = kind == 0.0, kind == 1.0
    density, energy = state[0, at], state[1, at]
    plastic, damage = state[5, at], state[6, at]
    pressure = (
        pick(first, second, tuple(c * c for c in sound_table))
        * (density - pick(first, second, rest_table))
        + pick(first, second, gruneisen_table) * density * energy
    )
    shear_dt = pick(first, second, tuple(2.0 * g for g in shear_table)) * dt
    trial = [state[7 + k, at] + shear_dt * strain[k] for k in range(6)]
    trial_sq = (
        trial[0] * trial[0]
        + trial[1] * trial[1]
        + trial[2] * trial[2]
        + 2.0 * (trial[3] * trial[3] + trial[4] * trial[4] + trial[5] * trial[5])
    )
    strain_sq = (
        strain[0] * strain[0]
        + strain[1] * strain[1]
        + strain[2] * strain[2]
        + 2.0 * (strain[3] * strain[3] + strain[4] * strain[4] + strain[5] * strain[5])
    )
    equivalent = jnp.sqrt(1.5 * trial_sq)
    strain_rate = jnp.sqrt(strain_sq * (2.0 / 3.0))
    hardened = pick(first, second, yield_table) + pick(first, second, harden_table) * jnp.exp(
        pick(first, second, exponent_table) * jnp.log(plastic)
    )
    flow = (
        hardened
        * (1.0 + pick(first, second, rate_table) * jnp.log(1.0 + strain_rate))
        * (1.0 - damage)
    )
    bound = jnp.maximum(equivalent, flow)
    per_bound = inverse(bound)
    factor = flow * per_bound
    increment = (bound - flow) * pick(first, second, tuple(1.0 / (3.0 * g) for g in shear_table))
    triaxial = jnp.clip(-pressure * per_bound, -1.5, 1.5)
    failure = 0.05 + 0.8 * jnp.exp(-1.5 * triaxial)
    rest[1, p] = jnp.where(ok, density * (plastic + increment), 0.0)
    worn = jnp.minimum(damage + increment * inverse(failure), 0.9)
    rest[2, p] = jnp.where(ok, density * worn, 0.0)
    dev = [jnp.where(ok, trial[k] * factor, 0.0) for k in range(6)]
    held = jnp.where(ok, pressure, 0.0)
    full = [dev[0] - held, dev[1] - held, dev[2] - held, dev[3], dev[4], dev[5]]
    for k in range(6):
        rest[3 + k, p] = density * dev[k]
        stress[k, p + 1] = full[k]
    work = (
        full[0] * grad[0][0]
        + full[1] * grad[1][1]
        + full[2] * grad[2][2]
        + 2.0 * (full[3] * strain[3] + full[4] * strain[4] + full[5] * strain[5])
    )
    rest[0, p] = jnp.where(ok, density * energy + dt * work, 0.0)
    return full


def force_at(dt, p, state, stress, lead, inside, ahead):
    density = state[0, p + PAD]
    here = [stress[k, p + 1] for k in range(6)]
    lead[0, p] = density
    for i in range(3):
        along_x, along_y, along_z = ACROSS[0][i], ACROSS[1][i], ACROSS[2][i]
        force = (
            central(ahead[along_x], stress[along_x, p])
            + central(roll(here[along_y], -1, 0), roll(here[along_y], 1, 0))
            + central(roll(here[along_z], -1, 1), roll(here[along_z], 1, 1))
        )
        pushed = jnp.where(inside[...] > 0.0, dt * force, 0.0)
        lead[1 + i, p] = density * state[2 + i, p + PAD] + pushed


def stress_and_force(dt, gather, state, stress, rest, lead, inside):
    zero = jnp.zeros((ROWS, LANES), jnp.float32)
    for k in range(6):
        stress[k, 0] = zero
    gather(0, 0, PAD)
    gather(0, 1, PAD + 1)

    def block(b, carry):
        for i in range(4):
            p = 4 * b + i
            full = strain_at(dt, p, state, stress, rest, inside)
            if i > 0:
                force_at(dt, p - 1, state, stress, lead, inside, full)
            else:
                force_at(dt, jnp.maximum(p - 1, 0), state, stress, lead, inside, full)
            soon = p + 2
            to = jnp.where(soon < PLANES, soon + PAD, PLANES + 2 * PAD - 1)
            gather(jnp.minimum(b + (i + 2) // 4, 3), (i + 2) % 4, to)
        return carry

    lax.fori_loop(0, PLANES // 4, block, 0)
    force_at(dt, PLANES - 1, state, stress, lead, inside, [zero] * 6)


def first_sweep(fields, f, moved, courants):
    here = fields[f, 0]
    ahead = fields[f, 1]
    fore = ahead - here
    slope = limited(here, fore)
    last_flux = None
    for p in range(PLANES - 1):
        further = fields[f, p + 2] if p + 2 < PLANES else 0.0
        next_fore = further - ahead
        next_slope = limited(fore, next_fore)
        courant = courants[p]
        flux = carried(courant > 0.0, here, ahead, slope, next_slope, courant, weigh(courant))
        moved[f, p] = here - (flux if last_flux is None else flux - last_flux)
        last_flux, here, ahead, fore, slope = flux, ahead, further, next_fore, next_slope
    moved[f, PLANES - 1] = here + last_flux


def first_courants(dt, lead, courants, inside):
    ok = inside[...] > 0.0
    here = None
    for p in range(PLANES):
        ahead = lead[1, p] * inverse(jnp.where(ok, lead[0, p], 1.0))
        if p > 0:
            courants[p - 1] = dt * 0.5 * (here + ahead)
        here = ahead


def second_sweep(moved, f, group, courant_of, mid):
    for i in range(GROUP):
        p = GROUP * group + i
        courant = courant_of(p)
        value = rolled_change(moved[f, p], courant > 0.0, courant, weigh(courant))
        mid[OWN * i : OWN * (i + 1)] = value[:OWN]


def turned(mid):
    value = mid[...].T
    return jnp.concatenate([value[: HALF + 8], value[LANES - 8 :]], axis=0)


def turn_back(value, put, f, group):
    gap = jnp.zeros((LANES - DEPTH, LANES), jnp.float32)
    value = jnp.concatenate([value[: HALF + 8], gap, value[HALF + 8 :]], axis=0).T
    for i in range(GROUP):
        put(f, GROUP * group + i, value[OWN * i : OWN * (i + 1)])


LEAD = 4
REST = 9
LEAD_AT = (0, 2, 3, 4)
REST_AT = (1, 5, 6, 7, 8, 9, 10, 11, 12)
ORDER = tuple((LEAD_AT + REST_AT).index(f) for f in range(FIELDS))


def sweep_lead(dt, lead, moved, mids, courants, scales, inside, face_y, face_z, put):
    along_x, along_y, along_z = courants
    first_courants(dt, lead, along_x, inside)
    for f in range(LEAD):
        first_sweep(lead, f, moved, along_x)

    def second_courant(p):
        density = jnp.where(inside[...] > 0.0, moved[0, p], 1.0)
        courant = rolled_courant(dt, density, moved[2, p], face_y[...])
        along_y[p] = courant
        return courant

    def second(group):
        second_sweep(moved, 0, group, second_courant, mids.at[group, 0])
        for f in range(1, LEAD):
            second_sweep(moved, f, group, lambda p: along_y[p], mids.at[group, f])

    def third(group):
        ok = face_z[0] > 0.0
        density = turned(mids.at[group, 0])
        momentum = turned(mids.at[group, 3])
        courant = rolled_courant(dt, jnp.where(ok, density, 1.0), momentum, face_z[1])
        along_z[group] = courant
        positive, weight = courant > 0.0, weigh(courant)
        value = rolled_change(density, positive, courant, weight)
        scale = jnp.where(ok, inverse(jnp.where(ok, value, 1.0)), 0.0)
        scales[group] = scale
        turn_back(jnp.where(ok, value, 0.0), put, 0, group)
        for f in range(1, LEAD):
            value = turned(mids.at[group, f]) if f < 3 else momentum
            turn_back(rolled_change(value, positive, courant, weight) * scale, put, f, group)

    second(0)
    second(1)
    third(0)
    third(1)


def sweep_rest(rest, moved, mids, courants, scales, put):
    along_x, along_y, along_z = courants
    last = REST - 1

    def second(f, group):
        second_sweep(moved, f, group, lambda p: along_y[p], mids.at[group])

    def field(f, carry):
        for group in range(2):
            courant = along_z[group]
            value = rolled_change(turned(mids.at[group]), courant > 0.0, courant, weigh(courant))
            turn_back(value * scales[group], put, f, group)
            second(jnp.minimum(f + 1, last), group)
        return carry

    def first(f, carry):
        first_sweep(rest, f, moved, along_x)
        return carry

    lax.fori_loop(0, REST, first, 0)
    for group in range(2):
        second(0, group)
    lax.fori_loop(0, REST, field, 0)


def clear_ends(state):
    zero = jnp.zeros((ROWS, LANES), jnp.float32)
    for f in range(FIELDS + 1):
        for p in (0, 1, PLANES + PAD, PLANES + PAD + 1):
            state[f, p] = zero


def lead_part(
    timestep, tops, own, sides, low, high, out, rest, along_x, along_y, along_z, scales, kinds, top,
    state, stress, lead, moved, mids, inside, face_y, face_z,
):
    set_masks(8, inside, face_y, face_z)
    clear_ends(state)
    dt = step_size(0, timestep, tops)

    def gather(block, i, to):
        j, odd = i // 2, i % 2
        p = 4 * block + i
        ok = inside[...] > 0.0
        lane = iota((ROWS, LANES), 1)
        group = lane >> 3
        around = []
        for which in range(2):
            at = MAIN_TILES + 8 * which + 2 * block + j
            tile = halo_tile(high[at], low[at], odd == 1)
            around.append(jnp.concatenate([sides[which, p], tile], axis=0))
        for f in range(FIELDS + 1):
            tile = roll(halo_tile(high[4 * f + block], low[4 * f + block], j == 1), HALF * odd, 1)
            value = jnp.concatenate([own[f, p], tile], axis=0)
            side = roll(jnp.where(group == f, around[1], around[0]), HALF - 8 * f, 1)
            value = jnp.where(ok, jnp.where(lane < HALF, value, side), 0.0)
            state[f, to] = value
            if f == FIELDS:
                kinds[p] = value

    stress_and_force(dt, gather, state, stress, rest, lead, inside)

    def put(f, p, value):
        out[f, p] = value

    sweep_lead(
        dt, lead, moved, mids, (along_x, along_y, along_z), scales, inside, face_y, face_z, put
    )

    def peaks(p, peak):
        speed = jnp.maximum(jnp.abs(out[1, p]), jnp.abs(out[2, p]))
        speed = jnp.maximum(speed, jnp.abs(out[3, p]))
        kind = kinds[p, :OWN]
        speed = speed + pick(kind == 0.0, kind == 1.0, sound_table)
        lane = iota((OWN, LANES), 1)
        return jnp.maximum(peak, jnp.where(lane < HALF, speed, 0.0))

    peak = lax.fori_loop(0, PLANES, peaks, jnp.zeros((OWN, LANES), jnp.float32))
    top[...] = jnp.full(top.shape, jnp.max(peak), jnp.float32)


def rest_part(lead, rest, along_x, along_y, along_z, scales, out, up, down, moved, mids):
    def put(f, p, value):
        out[f, p] = value

    sweep_rest(rest, moved, mids, (along_x, along_y, along_z), scales, put)

    def messages(i, carry):
        for f in range(FIELDS):
            src, at = (lead, LEAD_AT.index(f)) if f in LEAD_AT else (out, REST_AT.index(f))
            even, odd = src[at, 2 * i], src[at, 2 * i + 1]
            up[f, i] = stack_rows(even, odd, True)
            down[f, i] = stack_rows(even, odd, False)
        return carry

    lax.fori_loop(0, PLANES // 2, messages, 0)


def first_kernel(
    timestep, tops, own, sides, low, high, out, out_rest, kinds, top, up, down,
    rest, along_x, along_y, along_z, scales,
    state, stress, lead, moved, mids, inside, face_y, face_z, rest_moved, rest_mids,
):
    lead_part(
        timestep, tops, own, sides, low, high, out, rest, along_x, along_y, along_z, scales, kinds, top,
        state, stress, lead, moved, mids, inside, face_y, face_z,
    )
    rest_part(out, rest, along_x, along_y, along_z, scales, out_rest, up, down, rest_moved, rest_mids)


def second_kernel(
    timestep, tops, own_lead, own_rest, kinds, low, high, mine, to1, to2, to3,
    state, stress, lead, moved, mids, inside, face_y, face_z,
    rest, rest_moved, rest_mids, along_x, along_y, along_z, scales, out,
):
    set_masks(4, inside, face_y, face_z)
    clear_ends(state)
    dt = step_size(1, timestep, tops)

    def gather(block, i, to):
        p = 4 * block + i
        pair, odd = 2 * block + i // 2, i % 2
        ok = inside[...] > 0.0
        for f in range(FIELDS):
            src, at = (own_lead, LEAD_AT.index(f)) if f in LEAD_AT else (own_rest, REST_AT.index(f))
            tile = halo_tile(high[f, pair], low[f, pair], odd == 1)
            state[f, to] = jnp.where(ok, jnp.concatenate([src[at, p], tile], axis=0), 0.0)
        state[FIELDS, to] = kinds[p]

    stress_and_force(dt, gather, state, stress, rest, lead, inside)
    courants = (along_x, along_y, along_z)

    def put_lead(f, p, value):
        out[f, p] = value

    def put_rest(f, p, value):
        out[LEAD + f, p] = value

    sweep_lead(dt, lead, moved, mids, courants, scales, inside, face_y, face_z, put_lead)
    sweep_rest(rest, rest_moved, rest_mids, courants, scales, put_rest)
    me = position()[0]
    for k, part in enumerate((mine, to1, to2, to3)):
        pack_block(out, me ^ k, part)


def pack_block(out, block, part):
    left = iota((OWN, LANES), 1) < HALF
    first = 4 * block
    for f in range(FIELDS):
        for j in range(2):
            even, odd = out[ORDER[f], first + 2 * j], out[ORDER[f], first + 2 * j + 1]
            part[f, j] = jnp.where(left, even, roll(odd, HALF, 1))


def unpack_kernel(mine, from1, from2, from3, dens, ener, vel, plas, dama, devi, held):
    me = position()[0]
    refs = [dens, ener] + [vel.at[i] for i in range(3)] + [plas, dama]
    refs = refs + [devi.at[i] for i in range(6)]
    for k, src in enumerate((mine, from1, from2, from3)):
        held[me ^ k] = src[...]
    left = iota((OWN, LANES), 1) < HALF
    for f in range(FIELDS):
        for j in range(2):
            for t in range(2):
                first, second = held[2 * t, f, j], held[2 * t + 1, f, j]
                cols = slice(t * LANES, (t + 1) * LANES)
                refs[f][2 * j, :, cols] = jnp.where(left, first, roll(second, HALF, 1))
                refs[f][2 * j + 1, :, cols] = jnp.where(left, roll(first, HALF, 1), second)


IN_VMEM = pl.BlockSpec(memory_space=pltpu.VMEM)
IN_SMEM = pl.BlockSpec(memory_space=pltpu.SMEM)


def call(kernel, scalars, outs, scratch, *args, micros=1):
    return pl.pallas_call(
        kernel,
        out_shape=[jax.ShapeDtypeStruct(shape, jnp.float32) for shape in outs],
        in_specs=[IN_SMEM] * scalars + [IN_VMEM] * (len(args) - scalars),
        out_specs=[IN_VMEM] * len(outs),
        scratch_shapes=[pltpu.VMEM(shape, jnp.float32) for shape in scratch],
        compiler_params=pltpu.CompilerParams(vmem_limit_bytes=CALL_LIMIT),
        cost_estimate=pl.CostEstimate(flops=0, bytes_accessed=micros * 3_600_000, transcendentals=0),
    )(*args)


def ring_pair(to_next, to_last, axes, order):
    after = order[1:] + order[:1]
    low = lax.ppermute(to_next, axes, list(zip(order, after)))
    high = lax.ppermute(to_last, axes, list(zip(after, order)))
    return low, high


def swap_block(part, k):
    return lax.ppermute(part, "gx", [(i, i ^ k) for i in range(lax.axis_size("gx"))])


def swap_blocks(parts):
    return [swap_block(part, k + 1) for k, part in enumerate(parts)]


def shards(density, energy, velocity, plastic_strain, damage, deviator, materials, timestep):
    size_x, size_y, size_z = lax.axis_size("gx"), lax.axis_size("gy"), lax.axis_size("gz")
    all_fields = FIELDS + 1
    part = (PART_ROWS + 8, LANES)
    inputs = (density, energy, velocity, plastic_strain, damage, deviator, materials)
    edge = (4, OWN, LANES)
    own, *parts, edges, z_up, z_down = pl.pallas_call(
        pack_kernel,
        out_shape=[
            jax.ShapeDtypeStruct(shape, jnp.float32) for shape in [part] * 4 + [(4, 2) + edge, edge, edge]
        ],
        in_specs=[pl.BlockSpec(memory_space=pltpu.HBM)] * len(inputs),
        out_specs=[IN_VMEM] * 7,
        scratch_shapes=[pltpu.VMEM(array.shape, array.dtype) for array in inputs]
        + [pltpu.SemaphoreType.DMA((len(inputs),))],
        compiler_params=pltpu.CompilerParams(vmem_limit_bytes=PACK_LIMIT),
    )(*inputs)
    z_low, z_high = ring_pair(z_up, z_down, "gz", list(range(size_z)))
    parts = swap_blocks(parts)
    own_z, *z_parts = call(edge_kernel, 0, [(2,) + edge] * 4, [], edges, z_low, z_high)
    z_parts = swap_blocks(z_parts)
    message = (MAIN_TILES + PLANES, 8, LANES)
    state, sides, up, down, top = call(
        spread_kernel,
        0,
        [(all_fields, PLANES, OWN, LANES), (2, PLANES, OWN, LANES), message, message]
        + [(size_y * size_z, LANES)],
        [],
        own,
        *parts,
        own_z,
        *z_parts,
    )
    low, high = ring_pair(up, down, "gy", list(range(size_y)))
    tops = lax.all_to_all(top, ("gy", "gz"), 0, 0)
    full = (ROWS, LANES)
    scratch = [
        (all_fields, PLANES + 2 * PAD) + full,
        (6, PLANES + 2) + full,
        (LEAD, PLANES) + full,
        (LEAD, PLANES) + full,
        (2, LEAD, LANES, LANES),
        full,
        full,
        (2, DEPTH, LANES),
    ]
    left_over = [
        (REST, PLANES) + full,
        (PLANES - 1,) + full,
        (PLANES,) + full,
        (2, DEPTH, LANES),
        (2, DEPTH, LANES),
    ]
    rest_scratch = [(REST, PLANES) + full, (2, LANES, LANES)]
    lead, rest, kinds, top, up, down = call(
        first_kernel,
        1,
        [(LEAD, PLANES, OWN, LANES), (REST, PLANES, OWN, LANES), (PLANES,) + full]
        + [(size_x * size_y * size_z, LANES)]
        + [(FIELDS, PLANES // 2, 8, LANES)] * 2,
        left_over + scratch + rest_scratch,
        timestep,
        tops,
        state,
        sides,
        low,
        high,
    )
    low, high = ring_pair(up, down, "gy", list(range(size_y)))
    tops = lax.all_to_all(top, ("gx", "gy", "gz"), 0, 0)
    mine, *parts = call(
        second_kernel,
        1,
        [(FIELDS, 2, OWN, LANES)] * 4,
        scratch + left_over[:1] + rest_scratch + left_over[1:] + [(FIELDS, PLANES, OWN, LANES)],
        timestep,
        tops,
        lead,
        rest,
        kinds,
        low,
        high,
    )
    parts = swap_blocks(parts)
    cells = density.shape
    return tuple(
        call(
            unpack_kernel,
            0,
            [cells, cells, (3,) + cells, cells, cells, (6,) + cells],
            [(4, FIELDS, 2, OWN, LANES)],
            mine,
            *parts,
        )
    )


def solution(mesh):
    cells = P("gx", "gy", "gz")
    vectors = P(None, "gx", "gy", "gz")
    return jax.shard_map(
        shards,
        mesh=mesh,
        in_specs=(cells, cells, vectors, cells, cells, vectors, cells, P()),
        out_specs=(cells, cells, vectors, cells, cells, vectors),
        check_vma=False,
    )
```

```python
import jax
import jax.numpy as jnp
from jax import lax
from jax.experimental import pallas as pl
from jax.experimental.pallas import tpu as pltpu
from jax.sharding import PartitionSpec as P


FIELDS = 13
PLANES = 16
ROWS = 24
OWN = 16
LANES = 128
HALF = 64
DEPTH = 80
GROUP = 8
PAD = 2

shear_table = (1.0, 0.5, 0.8)
sound_table = (1.5, 1.2, 1.0)
gruneisen_table = (2.0, 2.1, 1.9)
rest_table = (4.0, 3.0, 5.0)
yield_table = (0.3, 0.2, 0.25)
harden_table = (0.5, 0.3, 0.4)
exponent_table = (0.3, 0.4, 0.35)
rate_table = (0.02, 0.015, 0.01)
cfl_number = 0.2

PACK_LIMIT = 62 * 1024 * 1024
CALL_LIMIT = 48 * 1024 * 1024
ACROSS = ((0, 3, 5), (3, 1, 4), (5, 4, 2))


def roll(value, shift, axis):
    shift = shift % value.shape[axis]
    return value if shift == 0 else pltpu.roll(value, shift, axis)


def position():
    size_x = lax.axis_size("gx")
    place_x = lax.axis_index("gx")
    chunk = lax.axis_index("gz") * size_x + place_x
    return place_x, lax.axis_index("gy"), chunk, lax.axis_size("gy") - 1, size_x * lax.axis_size("gz") - 1


def iota(shape, axis):
    return lax.broadcasted_iota(jnp.int32, shape, axis)


def inverse(value):
    return pltpu.reciprocal(value, approx=True)


def pick(first, second, table):
    return jnp.where(first, table[0], jnp.where(second, table[1], table[2]))


def stack_rows(even, odd, upper):
    low_rows = iota((8, LANES), 0) < 4
    if upper:
        return jnp.where(low_rows, roll(even[8:], 4, 0), odd[8:])
    return jnp.where(low_rows, even[:8], roll(odd[:8], 4, 0))


def halo_tile(high, low, odd):
    low_rows = iota((8, LANES), 0) < 4
    if odd:
        return jnp.where(low_rows, roll(high, 4, 0), low)
    return jnp.where(low_rows, high, roll(low, 4, 0))


PART_ROWS = (FIELDS + 1) * 2 * OWN


def part_rows(f, j):
    return slice((2 * f + j) * OWN, (2 * f + j + 1) * OWN)


def pack_kernel(*args):
    sources, (own, to1, to2, to3, edges, z_up, z_down) = args[:7], args[7:14]
    buffers, arrived = args[14:21], args[21]
    copies = [
        pltpu.make_async_copy(source, buffer, arrived.at[i])
        for i, (source, buffer) in enumerate(zip(sources, buffers))
    ]
    for i in (2, 6, 0, 1, 3, 4, 5):
        copies[i].start()
    dens, ener, vel, plas, dama, devi, mat = buffers
    me = position()[0]
    refs = [dens, ener] + [vel.at[i] for i in range(3)] + [plas, dama]
    refs = refs + [devi.at[i] for i in range(6)] + [mat]
    copies[2].wait()
    copies[6].wait()
    peak = None
    for x in range(4):
        for t in range(2):
            cols = slice(t * LANES, (t + 1) * LANES)
            speed = jnp.maximum(jnp.abs(vel[0, x, :, cols]), jnp.abs(vel[1, x, :, cols]))
            speed = jnp.maximum(speed, jnp.abs(vel[2, x, :, cols]))
            kind = mat[x, :, cols]
            speed = speed + pick(kind == 0, kind == 1, sound_table)
            peak = speed if peak is None else jnp.maximum(peak, speed)
    peak = jnp.full((8, LANES), jnp.max(peak), jnp.float32)
    for out in (own, to1, to2, to3):
        out[PART_ROWS:] = peak
    left = iota((OWN, LANES), 1) < HALF

    def pack(f):
        for k, out in enumerate((own, to1, to2, to3)):
            target = me ^ k
            cols = pl.ds(pl.multiple_of((target >> 1) * LANES, LANES), LANES)
            odd = target & 1
            side = left == (odd == 0)
            for j in range(2):
                even_plane = refs[f][2 * j, :, cols].astype(jnp.float32)
                odd_plane = refs[f][2 * j + 1, :, cols].astype(jnp.float32)
                stays = jnp.where(odd == 1, odd_plane, even_plane)
                turns = jnp.where(odd == 1, even_plane, odd_plane)
                out[part_rows(f, j)] = jnp.where(side, stays, roll(turns, HALF, 1))

    for f in (2, 3, 4, 13):
        pack(f)
    for copy, fields in ((0, (0,)), (1, (1,)), (3, (5,)), (4, (6,)), (5, range(7, 13))):
        copies[copy].wait()
        for f in fields:
            pack(f)

    group = iota((OWN, LANES), 1) >> 3

    def plane(x, carry):
        zero = jnp.zeros((OWN, LANES), jnp.float32)
        below, above = [zero] * 5, [zero] * 5
        for f in range(FIELDS + 1):
            in_below, in_above = group == (f + 7) % 16, group == f
            far_below, far_above = group == (f + 15) % 16, group == (f + 8) % 16
            for t in range(2):
                tile = refs[f][x, :, t * LANES : (t + 1) * LANES].astype(jnp.float32)
                tile = roll(tile, 8 * f, 1)
                below[2 * t + 1] = jnp.where(in_below, tile, below[2 * t + 1])
                below[2 * t + 2] = jnp.where(far_below, tile, below[2 * t + 2])
                above[2 * t] = jnp.where(in_above, tile, above[2 * t])
                above[2 * t + 1] = jnp.where(far_above, tile, above[2 * t + 1])
        for t in range(2):
            below[2 * t + 2] = roll(below[2 * t + 2], HALF, 1)
            above[2 * t + 1] = roll(above[2 * t + 1], HALF, 1)
        for g in range(4):
            edges[g, 0, x] = below[g]
            edges[g, 1, x] = above[g + 1]
        z_up[x] = below[4]
        z_down[x] = above[0]
        return carry

    lax.fori_loop(0, 4, plane, 0)


def edge_kernel(edges, from_below, from_above, own, to1, to2, to3):
    me = position()[0]
    for k, out in enumerate((own, to1, to2, to3)):
        target = me ^ k
        out[0] = jnp.where(target == 0, from_below[...], edges[target, 0])
        out[1] = jnp.where(target == 3, from_above[...], edges[target, 1])


MAIN_TILES = (FIELDS + 1) * 4


def spread_kernel(own, from1, from2, from3, own_z, z1, z2, z3, state, sides, up, down, top):
    me = position()[0]
    peak = jnp.maximum(
        jnp.maximum(own[PART_ROWS:], from1[PART_ROWS:]), jnp.maximum(from2[PART_ROWS:], from3[PART_ROWS:])
    )
    top[...] = jnp.broadcast_to(peak[:1], top.shape)
    for k, (src, side) in enumerate(((own, own_z), (from1, z1), (from2, z2), (from3, z3))):
        block = me ^ k
        for f in range(FIELDS + 1):
            first, second = src[part_rows(f, 0)], src[part_rows(f, 1)]
            state[f, 4 * block] = first
            state[f, 4 * block + 1] = roll(first, HALF, 1)
            state[f, 4 * block + 2] = second
            state[f, 4 * block + 3] = roll(second, HALF, 1)
            up[4 * f + block] = stack_rows(first, second, True)
            down[4 * f + block] = stack_rows(first, second, False)
        for which in range(2):
            for j in range(2):
                even, odd = side[which, 2 * j], side[which, 2 * j + 1]
                sides[which, 4 * block + 2 * j] = even
                sides[which, 4 * block + 2 * j + 1] = odd
                at = MAIN_TILES + 8 * which + 2 * block + j
                up[at] = stack_rows(even, odd, True)
                down[at] = stack_rows(even, odd, False)


def set_masks(width, inside, face_y, face_z):
    _, place_y, chunk, last_y, last_chunk = position()
    shape = (ROWS, LANES)
    row, lane = iota(shape, 0), iota(shape, 1)
    row_ok = (row < OWN) | ((row < OWN + 4) & (place_y < last_y)) | ((row >= OWN + 4) & (place_y > 0))
    lane_ok = (
        (lane < HALF)
        | ((lane < HALF + width) & (chunk < last_chunk))
        | ((lane >= LANES - width) & (chunk > 0))
    )
    ok = jnp.where(row_ok & lane_ok, 1.0, 0.0)
    inside[...] = ok
    face_y[...] = ok * roll(ok, -1, 0)
    row = iota((DEPTH, LANES), 0)
    row_ok = (
        (row < HALF)
        | ((row < HALF + width) & (chunk < last_chunk))
        | ((row >= DEPTH - width) & (chunk > 0))
    )
    ok = jnp.where(row_ok, 1.0, 0.0)
    face_z[0] = ok
    face_z[1] = ok * roll(ok, -1, 0)


def step_size(step_no, timestep, tops):
    top_speed = jnp.max(tops[...], axis=0, keepdims=True)
    asked = timestep[step_no]
    return asked / (1.0 + asked * top_speed / cfl_number)


def central(upper, lower):
    return 0.5 * (upper - lower)


def limited(back, fore):
    product = back * fore
    return jnp.where(product > 0.0, product * inverse(back + fore), 0.0)


def carried(positive, here, there, slope_here, slope_there, courant, weight):
    return courant * (
        jnp.where(positive, here, there) + weight * jnp.where(positive, slope_here, slope_there)
    )


def weigh(courant):
    return jnp.where(courant > 0.0, 1.0, -1.0) - courant


def rolled_change(q, positive, courant, weight):
    q_next = roll(q, -1, 0)
    fore = q_next - q
    slope = limited(roll(fore, 1, 0), fore)
    flux = carried(positive, q, q_next, slope, roll(slope, -1, 0), courant, weight)
    return q - (flux - roll(flux, 1, 0))


def rolled_courant(dt, density, momentum, closed):
    velocity = momentum * inverse(density)
    return dt * 0.5 * (velocity + roll(velocity, -1, 0)) * closed


def strain_at(dt, p, state, stress, rest, inside):
    at = p + PAD
    ok = inside[...] > 0.0
    vel = [state[2 + i, at] for i in range(3)]
    grad = [
        [
            central(state[2 + i, at + 1], state[2 + i, at - 1]),
            central(roll(vel[i], -1, 0), roll(vel[i], 1, 0)),
            central(roll(vel[i], -1, 1), roll(vel[i], 1, 1)),
        ]
        for i in range(3)
    ]
    third_div = (grad[0][0] + grad[1][1] + grad[2][2]) * (1.0 / 3.0)
    strain = [
        grad[0][0] - third_div,
        grad[1][1] - third_div,
        grad[2][2] - third_div,
        0.5 * (grad[0][1] + grad[1][0]),
        0.5 * (grad[1][2] + grad[2][1]),
        0.5 * (grad[0][2] + grad[2][0]),
    ]
    kind = state[FIELDS, at]
    first, second = kind == 0.0, kind == 1.0
    density, energy = state[0, at], state[1, at]
    plastic, damage = state[5, at], state[6, at]
    pressure = (
        pick(first, second, tuple(c * c for c in sound_table))
        * (density - pick(first, second, rest_table))
        + pick(first, second, gruneisen_table) * density * energy
    )
    shear_dt = pick(first, second, tuple(2.0 * g for g in shear_table)) * dt
    trial = [state[7 + k, at] + shear_dt * strain[k] for k in range(6)]
    trial_sq = (
        trial[0] * trial[0]
        + trial[1] * trial[1]
        + trial[2] * trial[2]
        + 2.0 * (trial[3] * trial[3] + trial[4] * trial[4] + trial[5] * trial[5])
    )
    strain_sq = (
        strain[0] * strain[0]
        + strain[1] * strain[1]
        + strain[2] * strain[2]
        + 2.0 * (strain[3] * strain[3] + strain[4] * strain[4] + strain[5] * strain[5])
    )
    equivalent = jnp.sqrt(1.5 * trial_sq)
    strain_rate = jnp.sqrt(strain_sq * (2.0 / 3.0))
    hardened = pick(first, second, yield_table) + pick(first, second, harden_table) * jnp.exp(
        pick(first, second, exponent_table) * jnp.log(plastic)
    )
    flow = (
        hardened
        * (1.0 + pick(first, second, rate_table) * jnp.log(1.0 + strain_rate))
        * (1.0 - damage)
    )
    bound = jnp.maximum(equivalent, flow)
    per_bound = inverse(bound)
    factor = flow * per_bound
    increment = (bound - flow) * pick(first, second, tuple(1.0 / (3.0 * g) for g in shear_table))
    triaxial = jnp.clip(-pressure * per_bound, -1.5, 1.5)
    failure = 0.05 + 0.8 * jnp.exp(-1.5 * triaxial)
    rest[1, p] = jnp.where(ok, density * (plastic + increment), 0.0)
    worn = jnp.minimum(damage + increment * inverse(failure), 0.9)
    rest[2, p] = jnp.where(ok, density * worn, 0.0)
    dev = [jnp.where(ok, trial[k] * factor, 0.0) for k in range(6)]
    held = jnp.where(ok, pressure, 0.0)
    full = [dev[0] - held, dev[1] - held, dev[2] - held, dev[3], dev[4], dev[5]]
    for k in range(6):
        rest[3 + k, p] = density * dev[k]
        stress[k, p + 1] = full[k]
    work = (
        full[0] * grad[0][0]
        + full[1] * grad[1][1]
        + full[2] * grad[2][2]
        + 2.0 * (full[3] * strain[3] + full[4] * strain[4] + full[5] * strain[5])
    )
    rest[0, p] = jnp.where(ok, density * energy + dt * work, 0.0)
    return full


def force_at(dt, p, state, stress, lead, inside, ahead):
    density = state[0, p + PAD]
    here = [stress[k, p + 1] for k in range(6)]
    lead[0, p] = density
    for i in range(3):
        along_x, along_y, along_z = ACROSS[0][i], ACROSS[1][i], ACROSS[2][i]
        force = (
            central(ahead[along_x], stress[along_x, p])
            + central(roll(here[along_y], -1, 0), roll(here[along_y], 1, 0))
            + central(roll(here[along_z], -1, 1), roll(here[along_z], 1, 1))
        )
        pushed = jnp.where(inside[...] > 0.0, dt * force, 0.0)
        lead[1 + i, p] = density * state[2 + i, p + PAD] + pushed


def stress_and_force(dt, gather, state, stress, rest, lead, inside):
    zero = jnp.zeros((ROWS, LANES), jnp.float32)
    for k in range(6):
        stress[k, 0] = zero
    gather(0, 0, PAD)
    gather(0, 1, PAD + 1)

    def block(b, carry):
        for i in range(4):
            p = 4 * b + i
            full = strain_at(dt, p, state, stress, rest, inside)
            if i > 0:
                force_at(dt, p - 1, state, stress, lead, inside, full)
            else:
                force_at(dt, jnp.maximum(p - 1, 0), state, stress, lead, inside, full)
            soon = p + 2
            to = jnp.where(soon < PLANES, soon + PAD, PLANES + 2 * PAD - 1)
            gather(jnp.minimum(b + (i + 2) // 4, 3), (i + 2) % 4, to)
        return carry

    lax.fori_loop(0, PLANES // 4, block, 0)
    force_at(dt, PLANES - 1, state, stress, lead, inside, [zero] * 6)


def first_sweep(fields, f, moved, courants):
    here = fields[f, 0]
    ahead = fields[f, 1]
    fore = ahead - here
    slope = limited(here, fore)
    last_flux = None
    for p in range(PLANES - 1):
        further = fields[f, p + 2] if p + 2 < PLANES else 0.0
        next_fore = further - ahead
        next_slope = limited(fore, next_fore)
        courant = courants[p]
        flux = carried(courant > 0.0, here, ahead, slope, next_slope, courant, weigh(courant))
        moved[f, p] = here - (flux if last_flux is None else flux - last_flux)
        last_flux, here, ahead, fore, slope = flux, ahead, further, next_fore, next_slope
    moved[f, PLANES - 1] = here + last_flux


def first_courants(dt, lead, courants, inside):
    ok = inside[...] > 0.0
    here = None
    for p in range(PLANES):
        ahead = lead[1, p] * inverse(jnp.where(ok, lead[0, p], 1.0))
        if p > 0:
            courants[p - 1] = dt * 0.5 * (here + ahead)
        here = ahead


def second_sweep(moved, f, group, courant_of, mid):
    for i in range(GROUP):
        p = GROUP * group + i
        courant = courant_of(p)
        value = rolled_change(moved[f, p], courant > 0.0, courant, weigh(courant))
        mid[OWN * i : OWN * (i + 1)] = value[:OWN]


def turned(mid):
    value = mid[...].T
    return jnp.concatenate([value[: HALF + 8], value[LANES - 8 :]], axis=0)


def turn_twice(value, put, f, group):
    value = jnp.concatenate([value[:HALF], value[:HALF]], axis=0).T
    for i in range(GROUP):
        put(f, GROUP * group + i, value[OWN * i : OWN * (i + 1)])


def turn_back(value, put, f, group):
    gap = jnp.zeros((LANES - DEPTH, LANES), jnp.float32)
    value = jnp.concatenate([value[: HALF + 8], gap, value[HALF + 8 :]], axis=0).T
    for i in range(GROUP):
        put(f, GROUP * group + i, value[OWN * i : OWN * (i + 1)])


LEAD = 4
REST = 9
LEAD_AT = (0, 2, 3, 4)
REST_AT = (1, 5, 6, 7, 8, 9, 10, 11, 12)
ORDER = tuple((LEAD_AT + REST_AT).index(f) for f in range(FIELDS))


def sweep_lead(dt, lead, moved, mids, courants, scales, inside, face_y, face_z, put, back):
    along_x, along_y, along_z = courants
    first_courants(dt, lead, along_x, inside)
    for f in range(LEAD):
        first_sweep(lead, f, moved, along_x)

    def second_courant(p):
        density = jnp.where(inside[...] > 0.0, moved[0, p], 1.0)
        courant = rolled_courant(dt, density, moved[2, p], face_y[...])
        along_y[p] = courant
        return courant

    def second(group):
        second_sweep(moved, 0, group, second_courant, mids.at[group, 0])
        for f in range(1, LEAD):
            second_sweep(moved, f, group, lambda p: along_y[p], mids.at[group, f])

    def third(group):
        ok = face_z[0] > 0.0
        density = turned(mids.at[group, 0])
        momentum = turned(mids.at[group, 3])
        courant = rolled_courant(dt, jnp.where(ok, density, 1.0), momentum, face_z[1])
        along_z[group] = courant
        positive, weight = courant > 0.0, weigh(courant)
        value = rolled_change(density, positive, courant, weight)
        scale = jnp.where(ok, inverse(jnp.where(ok, value, 1.0)), 0.0)
        scales[group] = scale
        back(jnp.where(ok, value, 0.0), put, 0, group)
        for f in range(1, LEAD):
            value = turned(mids.at[group, f]) if f < 3 else momentum
            back(rolled_change(value, positive, courant, weight) * scale, put, f, group)

    second(0)
    second(1)
    third(0)
    third(1)


def sweep_rest(rest, moved, mids, courants, scales, put, back):
    along_x, along_y, along_z = courants
    last = REST - 1

    def second(f, group):
        second_sweep(moved, f, group, lambda p: along_y[p], mids.at[group])

    def field(f, carry):
        for group in range(2):
            courant = along_z[group]
            value = rolled_change(turned(mids.at[group]), courant > 0.0, courant, weigh(courant))
            back(value * scales[group], put, f, group)
            second(jnp.minimum(f + 1, last), group)
        return carry

    def first(f, carry):
        first_sweep(rest, f, moved, along_x)
        return carry

    lax.fori_loop(0, REST, first, 0)
    for group in range(2):
        second(0, group)
    lax.fori_loop(0, REST, field, 0)


def clear_ends(state):
    zero = jnp.zeros((ROWS, LANES), jnp.float32)
    for f in range(FIELDS + 1):
        for p in (0, 1, PLANES + PAD, PLANES + PAD + 1):
            state[f, p] = zero


def lead_part(
    timestep, tops, own, sides, low, high, out, rest, along_x, along_y, along_z, scales, kinds, top,
    state, stress, lead, moved, mids, inside, face_y, face_z,
):
    set_masks(8, inside, face_y, face_z)
    clear_ends(state)
    dt = step_size(0, timestep, tops)

    def gather(block, i, to):
        j, odd = i // 2, i % 2
        p = 4 * block + i
        ok = inside[...] > 0.0
        lane = iota((ROWS, LANES), 1)
        group = lane >> 3
        around = []
        for which in range(2):
            at = MAIN_TILES + 8 * which + 2 * block + j
            tile = halo_tile(high[at], low[at], odd == 1)
            around.append(jnp.concatenate([sides[which, p], tile], axis=0))
        for f in range(FIELDS + 1):
            tile = roll(halo_tile(high[4 * f + block], low[4 * f + block], j == 1), HALF * odd, 1)
            value = jnp.concatenate([own[f, p], tile], axis=0)
            side = roll(jnp.where(group == f, around[1], around[0]), HALF - 8 * f, 1)
            value = jnp.where(ok, jnp.where(lane < HALF, value, side), 0.0)
            state[f, to] = value
            if f == FIELDS:
                kinds[p] = value

    stress_and_force(dt, gather, state, stress, rest, lead, inside)

    def put(f, p, value):
        out[f, p] = value

    sweep_lead(
        dt, lead, moved, mids, (along_x, along_y, along_z), scales, inside, face_y, face_z, put, turn_back
    )

    def peaks(p, peak):
        speed = jnp.maximum(jnp.abs(out[1, p]), jnp.abs(out[2, p]))
        speed = jnp.maximum(speed, jnp.abs(out[3, p]))
        kind = kinds[p, :OWN]
        speed = speed + pick(kind == 0.0, kind == 1.0, sound_table)
        lane = iota((OWN, LANES), 1)
        return jnp.maximum(peak, jnp.where(lane < HALF, speed, 0.0))

    peak = lax.fori_loop(0, PLANES, peaks, jnp.zeros((OWN, LANES), jnp.float32))
    top[...] = jnp.full(top.shape, jnp.max(peak), jnp.float32)


def rest_part(lead, rest, along_x, along_y, along_z, scales, out, up, down, moved, mids):
    def put(f, p, value):
        out[f, p] = value

    sweep_rest(rest, moved, mids, (along_x, along_y, along_z), scales, put, turn_back)

    def messages(i, carry):
        for f in range(FIELDS):
            src, at = (lead, LEAD_AT.index(f)) if f in LEAD_AT else (out, REST_AT.index(f))
            even, odd = src[at, 2 * i], src[at, 2 * i + 1]
            up[f, i] = stack_rows(even, odd, True)
            down[f, i] = stack_rows(even, odd, False)
        return carry

    lax.fori_loop(0, PLANES // 2, messages, 0)


def second_kernel(
    timestep, tops, own_lead, own_rest, kinds, low, high, mine, to1, to2, to3,
    state, stress, lead, moved, mids, inside, face_y, face_z,
    rest, rest_moved, rest_mids, along_x, along_y, along_z, scales, out,
):
    set_masks(4, inside, face_y, face_z)
    clear_ends(state)
    dt = step_size(1, timestep, tops)

    def gather(block, i, to):
        p = 4 * block + i
        pair, odd = 2 * block + i // 2, i % 2
        ok = inside[...] > 0.0
        for f in range(FIELDS):
            src, at = (own_lead, LEAD_AT.index(f)) if f in LEAD_AT else (own_rest, REST_AT.index(f))
            tile = halo_tile(high[f, pair], low[f, pair], odd == 1)
            state[f, to] = jnp.where(ok, jnp.concatenate([src[at, p], tile], axis=0), 0.0)
        state[FIELDS, to] = kinds[p]

    stress_and_force(dt, gather, state, stress, rest, lead, inside)
    courants = (along_x, along_y, along_z)

    def put_lead(f, p, value):
        out[f, p] = value

    def put_rest(f, p, value):
        out[LEAD + f, p] = value

    sweep_lead(dt, lead, moved, mids, courants, scales, inside, face_y, face_z, put_lead, turn_twice)
    sweep_rest(rest, rest_moved, rest_mids, courants, scales, put_rest, turn_twice)
    me = position()[0]
    for k, part in enumerate((mine, to1, to2, to3)):
        pack_block(out, me ^ k, part)


def pack_block(out, block, part):
    left = iota((OWN, LANES), 1) < HALF
    first = 4 * block
    for f in range(FIELDS):
        for j in range(2):
            even, odd = out[ORDER[f], first + 2 * j], out[ORDER[f], first + 2 * j + 1]
            part[f, j] = jnp.where(left, even, odd)


def unpack_kernel(mine, from1, from2, from3, dens, ener, vel, plas, dama, devi, held):
    me = position()[0]
    refs = [dens, ener] + [vel.at[i] for i in range(3)] + [plas, dama]
    refs = refs + [devi.at[i] for i in range(6)]
    for k, src in enumerate((mine, from1, from2, from3)):
        held[me ^ k] = src[...]
    left = iota((OWN, LANES), 1) < HALF
    for f in range(FIELDS):
        for j in range(2):
            for t in range(2):
                first, second = held[2 * t, f, j], held[2 * t + 1, f, j]
                cols = slice(t * LANES, (t + 1) * LANES)
                refs[f][2 * j, :, cols] = jnp.where(left, first, roll(second, HALF, 1))
                refs[f][2 * j + 1, :, cols] = jnp.where(left, roll(first, HALF, 1), second)


IN_VMEM = pl.BlockSpec(memory_space=pltpu.VMEM)
IN_SMEM = pl.BlockSpec(memory_space=pltpu.SMEM)


def call(kernel, scalars, outs, scratch, *args, micros=1):
    return pl.pallas_call(
        kernel,
        out_shape=[jax.ShapeDtypeStruct(shape, jnp.float32) for shape in outs],
        in_specs=[IN_SMEM] * scalars + [IN_VMEM] * (len(args) - scalars),
        out_specs=[IN_VMEM] * len(outs),
        scratch_shapes=[pltpu.VMEM(shape, jnp.float32) for shape in scratch],
        compiler_params=pltpu.CompilerParams(vmem_limit_bytes=CALL_LIMIT),
        cost_estimate=pl.CostEstimate(flops=0, bytes_accessed=micros * 3_600_000, transcendentals=0),
    )(*args)


def ring_pair(to_next, to_last, axes, order):
    after = order[1:] + order[:1]
    low = lax.ppermute(to_next, axes, list(zip(order, after)))
    high = lax.ppermute(to_last, axes, list(zip(after, order)))
    return low, high


def swap_block(part, k):
    return lax.ppermute(part, "gx", [(i, i ^ k) for i in range(lax.axis_size("gx"))])


def swap_blocks(parts):
    return [swap_block(part, k + 1) for k, part in enumerate(parts)]


def shards(density, energy, velocity, plastic_strain, damage, deviator, materials, timestep):
    size_x, size_y, size_z = lax.axis_size("gx"), lax.axis_size("gy"), lax.axis_size("gz")
    all_fields = FIELDS + 1
    part = (PART_ROWS + 8, LANES)
    inputs = (density, energy, velocity, plastic_strain, damage, deviator, materials)
    edge = (4, OWN, LANES)
    own, *parts, edges, z_up, z_down = pl.pallas_call(
        pack_kernel,
        out_shape=[
            jax.ShapeDtypeStruct(shape, jnp.float32) for shape in [part] * 4 + [(4, 2) + edge, edge, edge]
        ],
        in_specs=[pl.BlockSpec(memory_space=pltpu.HBM)] * len(inputs),
        out_specs=[IN_VMEM] * 7,
        scratch_shapes=[pltpu.VMEM(array.shape, array.dtype) for array in inputs]
        + [pltpu.SemaphoreType.DMA((len(inputs),))],
        compiler_params=pltpu.CompilerParams(vmem_limit_bytes=PACK_LIMIT),
    )(*inputs)
    z_low, z_high = ring_pair(z_up, z_down, "gz", list(range(size_z)))
    parts = swap_blocks(parts)
    own_z, *z_parts = call(edge_kernel, 0, [(2,) + edge] * 4, [], edges, z_low, z_high)
    z_parts = swap_blocks(z_parts)
    message = (MAIN_TILES + PLANES, 8, LANES)
    state, sides, up, down, top = call(
        spread_kernel,
        0,
        [(all_fields, PLANES, OWN, LANES), (2, PLANES, OWN, LANES), message, message]
        + [(size_y * size_z, LANES)],
        [],
        own,
        *parts,
        own_z,
        *z_parts,
    )
    low, high = ring_pair(up, down, "gy", list(range(size_y)))
    tops = lax.all_to_all(top, ("gy", "gz"), 0, 0)
    full = (ROWS, LANES)
    scratch = [
        (all_fields, PLANES + 2 * PAD) + full,
        (6, PLANES + 2) + full,
        (LEAD, PLANES) + full,
        (LEAD, PLANES) + full,
        (2, LEAD, LANES, LANES),
        full,
        full,
        (2, DEPTH, LANES),
    ]
    left_over = [
        (REST, PLANES) + full,
        (PLANES - 1,) + full,
        (PLANES,) + full,
        (2, DEPTH, LANES),
        (2, DEPTH, LANES),
    ]
    rest_scratch = [(REST, PLANES) + full, (2, LANES, LANES)]
    lead, *rest, kinds, top = call(
        lead_part,
        1,
        [(LEAD, PLANES, OWN, LANES)] + left_over + [(PLANES,) + full, (size_x * size_y * size_z, LANES)],
        scratch,
        timestep,
        tops,
        state,
        sides,
        low,
        high,
    )
    tops = lax.all_to_all(top, ("gx", "gy", "gz"), 0, 0)
    rest, up, down = call(
        rest_part,
        0,
        [(REST, PLANES, OWN, LANES)] + [(FIELDS, PLANES // 2, 8, LANES)] * 2,
        rest_scratch,
        lead,
        *rest,
        micros=20,
    )
    tops, up, down = lax.optimization_barrier((tops, up, down))
    low, high = ring_pair(up, down, "gy", list(range(size_y)))
    mine, *parts = call(
        second_kernel,
        1,
        [(FIELDS, 2, OWN, LANES)] * 4,
        scratch + left_over[:1] + rest_scratch + left_over[1:] + [(FIELDS, PLANES, OWN, LANES)],
        timestep,
        tops,
        lead,
        rest,
        kinds,
        low,
        high,
    )
    parts = swap_blocks(parts)
    cells = density.shape
    return tuple(
        call(
            unpack_kernel,
            0,
            [cells, cells, (3,) + cells, cells, cells, (6,) + cells],
            [(4, FIELDS, 2, OWN, LANES)],
            mine,
            *parts,
        )
    )


def solution(mesh):
    cells = P("gx", "gy", "gz")
    vectors = P(None, "gx", "gy", "gz")
    return jax.shard_map(
        shards,
        mesh=mesh,
        in_specs=(cells, cells, vectors, cells, cells, vectors, cells, P()),
        out_specs=(cells, cells, vectors, cells, cells, vectors),
        check_vma=False,
    )
```
